32 devices in a mesh: ctx: 8 (over y, x, core), ch: 4 (over z).
Axes of the slice: x: 2, y: 2, z: 4, core: 2. Of those that a mesh axis runs over, the one named last changes fastest.
Arguments:
- query_proj: bfloat16 [16384, 4096], P('ctx', 'ch'), may hold values from -6 to 6
- key_proj: bfloat16 [16384, 4096], P('ctx', 'ch'), may hold values from -6 to 6
- value_proj: bfloat16 [16384, 4096], P('ctx', 'ch'), may hold values from -6 to 6
- out_grad: bfloat16 [16384, 4096], P('ctx', 'ch'), may hold values from -6 to 6
- long_filter: bfloat16 [4096, 16384], P(None, ('ch', 'ctx')), as said below
- skip_gain: float32 [4096], P('ch'), may hold values from -4 to 4
Outputs:
- output: bfloat16 [16384, 4096], P('ctx', 'ch')
- query_grad: bfloat16 [16384, 4096], P('ctx', 'ch')
- key_grad: bfloat16 [16384, 4096], P('ctx', 'ch')
- value_grad: bfloat16 [16384, 4096], P('ctx', 'ch')
The draws below stay inside these ranges and needn't reach their ends.
Inputs may be any that keep to these rules, and one draw needn't show every extreme that they name: `long_filter`: each channel's filter is a rough sequence of taps under an envelope that falls with the tap index.
All inputs are finite; a program needn't handle non-finite values.
Results may differ from the reference program's by a relative error of at most 0.007.
Values may be sent and summed in bfloat16 or wider, within the bound.
No kernel may reach another device: no remote copies, remote signals or barrier semaphores. Data moves between devices by JAX's collectives and lax.ppermute only.
A program may use at most 384 MiB of HBM per device.

```python
import math
import jax
import jax.numpy as jnp
from jax import lax

C = 4096
L = 16384


def draw_long_filter(key, part):
    keys = jax.random.split(key, 5)
    tap_index = jnp.arange(L, dtype=jnp.int32)[None, :]
    tap_float = tap_index.astype(jnp.float32)
    rough = jax.random.normal(keys[0], (C, L), jnp.float32)
    reach = jnp.exp(jax.random.uniform(keys[1], (C, 1), jnp.float32, math.log(20.0), math.log(4.0 * L)))
    envelope = jnp.exp(-tap_float / reach)
    spots = jax.random.randint(keys[2], (C, 3), 0, L)
    drops = jax.random.uniform(keys[3], (C, 3), jnp.float32, 0.5, 0.8)
    for index in range(3):
        envelope = envelope * jnp.where(tap_index >= spots[:, index:index + 1], drops[:, index:index + 1], 1.0)
    floor_level = jax.random.uniform(keys[4], (C, 1), jnp.float32, 0.4, 0.7)
    envelope = envelope + floor_level * jnp.exp(-tap_float / (2.0 * L))
    scale = jnp.sqrt(jnp.sum(envelope * envelope, axis=1, keepdims=True))
    return (rough * envelope / scale).astype(jnp.bfloat16)


def block_levels(key, shape, cuts, smallest, high):
    loudness, own = 1.0, jax.random.fold_in(key, 6)
    for dim, parts in cuts:
        draws = jnp.exp(jax.random.uniform(jax.random.fold_in(own, dim), (parts,), jnp.float32, smallest / len(cuts), high / len(cuts)))
        loudness = loudness * jnp.repeat(draws, shape[dim] // parts).reshape([-1 if axis == dim else 1 for axis in range(len(shape))])
    return loudness


def scatter_about(stream_key, dims, width, most, cuts=(), kind=jnp.bfloat16):
    level = block_levels(stream_key, dims, cuts, -0.22, 0.18) if cuts else 1.0
    entries = jax.random.normal(stream_key, dims, jnp.float32) * width * level
    return jnp.minimum(jnp.maximum(entries, -most), most).astype(kind)


def setup_inputs(seed: int = 0) -> dict:
    splits = jax.random.split(jax.random.key(seed), 7)
    query_proj = scatter_about(splits[0], (L, C), 1.0, 6.0, ((0, 8), (1, 4)))
    key_proj = scatter_about(splits[1], (L, C), 1.0, 6.0, ((0, 8), (1, 4)))
    value_proj = scatter_about(splits[2], (L, C), 1.0, 6.0, ((0, 8), (1, 4)))
    out_grad = scatter_about(splits[3], (L, C), 1.0, 6.0, ((0, 8), (1, 4)))
    long_filter = draw_long_filter(jax.random.fold_in(splits[6], 71), 0)
    skip_gain = scatter_about(splits[5], (C,), 1.0, 4.0, ((0, 4),), jnp.float32)
    return dict(query_proj=query_proj, key_proj=key_proj, value_proj=value_proj, out_grad=out_grad, long_filter=long_filter, skip_gain=skip_gain)


def convolve_block(operands):
    filters, forward_in, backward_in = operands
    points = 2 * L
    spectrum = jnp.fft.rfft(filters.astype(jnp.float32), n=points, axis=1)
    causal_out = jnp.fft.irfft(jnp.fft.rfft(forward_in.astype(jnp.float32), n=points, axis=1) * spectrum, n=points, axis=1)[:, :L]
    adjoint_out = jnp.fft.irfft(jnp.fft.rfft(backward_in.astype(jnp.float32), n=points, axis=1) * jnp.conj(spectrum), n=points, axis=1)[:, :L]
    return causal_out.astype(jnp.bfloat16), adjoint_out.astype(jnp.bfloat16)


def reference(query_proj, key_proj, value_proj, out_grad, long_filter, skip_gain):
    gated_kv = (key_proj.astype(jnp.float32) * value_proj.astype(jnp.float32)).astype(jnp.bfloat16)
    grad_gate = (out_grad.astype(jnp.float32) * query_proj.astype(jnp.float32)).astype(jnp.bfloat16)
    block_rows = min(64, C)
    blocks = C // block_rows
    filters = long_filter.reshape(blocks, block_rows, L)
    forward_in = gated_kv.T.reshape(blocks, block_rows, L)
    backward_in = grad_gate.T.reshape(blocks, block_rows, L)
    convolved, reflected = lax.map(convolve_block, (filters, forward_in, backward_in))
    convolved = convolved.reshape(C, L).T
    reflected = reflected.reshape(C, L).T
    summed = convolved.astype(jnp.float32) + skip_gain[None, :] * gated_kv.astype(jnp.float32)
    output = (query_proj.astype(jnp.float32) * summed).astype(jnp.bfloat16)
    query_grad = (out_grad.astype(jnp.float32) * summed).astype(jnp.bfloat16)
    grad_sum = reflected.astype(jnp.float32) + skip_gain[None, :] * grad_gate.astype(jnp.float32)
    key_grad = (grad_sum * value_proj.astype(jnp.float32)).astype(jnp.bfloat16)
    value_grad = (grad_sum * key_proj.astype(jnp.float32)).astype(jnp.bfloat16)
    return output, query_grad, key_grad, value_grad
```

```python
import functools
import math

import jax
import jax.numpy as jnp
import ml_dtypes
import numpy as np
from jax import lax
from jax.experimental import pallas as pl
from jax.experimental.pallas import tpu as pltpu
from jax.sharding import PartitionSpec as P

LANES = 128
TILE = 16
VMEM_BYTES = 56 * 1024 * 1024

f32 = jnp.float32
bf16 = jnp.bfloat16


def two_parts(matrix):
    high = matrix.astype(ml_dtypes.bfloat16)
    low = (matrix - high.astype(np.float64)).astype(ml_dtypes.bfloat16)
    return high, low


def make_tables(rows):
    points = rows * LANES
    n1, k1 = np.arange(rows), np.arange(rows)
    n2, k2 = np.arange(LANES), np.arange(LANES)
    lead = 2 * math.pi / rows * np.outer(k1 + 0.25, n1)
    twist = 2 * math.pi / points * np.outer(k1 + 0.25, n2)
    trail = 2 * math.pi / LANES * np.outer(n2, k2)
    lead_fwd = np.concatenate([np.cos(lead), -np.sin(lead)], 0)
    lead_inv = np.concatenate([np.cos(lead).T, -np.sin(lead).T], 1) / points
    cosine, sine = np.cos(trail), np.sin(trail)
    trail_fwd = np.block([[cosine, -sine], [sine, cosine]])
    trail_inv = np.block([[cosine, sine], [-sine, cosine]])
    lead_fwd = np.concatenate(two_parts(lead_fwd), 1)
    lead_inv = np.concatenate(two_parts(lead_inv), 0)
    trail_fwd = np.stack(two_parts(trail_fwd))
    trail_inv = np.stack(two_parts(trail_inv))
    twist = np.stack([np.cos(twist), -np.sin(twist)]).astype(np.float32)
    return lead_fwd, lead_inv, trail_fwd, trail_inv, twist


def dot(left, right):
    return jnp.dot(left, right, preferred_element_type=f32)


def split(value):
    high = value.astype(bf16)
    return high, (value - high.astype(f32)).astype(bf16)


def lead_stage(lead, twist, pair):
    rows = pair.shape[0]
    turned = dot(lead, jnp.concatenate([pair, pair], 0))
    real, imag = turned[:rows], turned[rows:]
    parts = []
    for side in range(2):
        lanes = slice(side * LANES, (side + 1) * LANES)
        re, im = real[:, lanes], imag[:, lanes]
        parts.append(
            jnp.concatenate([re * twist[0] - im * twist[1], re * twist[1] + im * twist[0]], 1)
        )
    return parts


def trail_stage(high, low, matrix_ref):
    return dot(high, matrix_ref[0]) + dot(low, matrix_ref[0]) + dot(high, matrix_ref[1])


def spectrum_kernel(pieces, group, lead_ref, trail_ref, twist_ref, *refs):
    taps = refs[:pieces]
    out_ref, scratch, high, low = refs[pieces:]
    sources, _, _, width = taps[0].shape
    count = pieces * sources
    for piece in range(pieces):
        for source in range(sources):
            row = (piece * sources + source) * group
            for part in range(width // LANES):
                lanes = slice(part * LANES, (part + 1) * LANES)
                scratch[part, row : row + group, :] = taps[piece][source, 0, :, lanes].astype(f32)
    lead, twist = lead_ref[...], (twist_ref[0], twist_ref[1])
    rows = count * (width // LANES)

    def channel(index):
        parts = [
            scratch[part, pl.ds(index, count, stride=group), :] for part in range(width // LANES)
        ]
        return jnp.concatenate(parts, 0).astype(bf16)

    for index in range(0, group, 2):
        pair = jnp.concatenate([channel(index), channel(index + 1)], 1)
        for side, value in enumerate(lead_stage(lead, twist, pair)):
            place = slice((index + side) * rows, (index + side + 1) * rows)
            high[place, :], low[place, :] = split(value)
    out_ref[...] = trail_stage(high[...], low[...], trail_ref).reshape(out_ref.shape)


def filter_spectrum(pieces, lead, trail, twist, group):
    sources, outer, inner, width = pieces[0].shape
    rows = lead.shape[1] // 2
    steps = inner // group
    whole = lambda ndim: (lambda *_: (0,) * ndim)
    return pl.pallas_call(
        functools.partial(spectrum_kernel, len(pieces), group),
        out_shape=jax.ShapeDtypeStruct((outer * inner, rows, 2 * LANES), f32),
        grid=(outer * steps,),
        in_specs=[
            pl.BlockSpec(lead.shape, whole(2)),
            pl.BlockSpec(trail.shape, whole(3)),
            pl.BlockSpec(twist.shape, whole(3)),
        ]
        + [
            pl.BlockSpec(
                (sources, 1, group, width), lambda step: (0, step // steps, step % steps, 0)
            )
        ]
        * len(pieces),
        out_specs=pl.BlockSpec((group, rows, 2 * LANES), lambda step: (step, 0, 0)),
        scratch_shapes=[
            pltpu.VMEM((width // LANES, len(pieces) * sources * group, LANES), f32),
            pltpu.VMEM((group * rows, 2 * LANES), bf16),
            pltpu.VMEM((group * rows, 2 * LANES), bf16),
        ],
        compiler_params=pltpu.CompilerParams(vmem_limit_bytes=VMEM_BYTES),
        cost_estimate=pl.CostEstimate(
            flops=outer * inner * 10**6, bytes_accessed=2**20, transcendentals=0
        ),
        name="filter_spectrum",
    )(lead, trail, twist, *pieces)


def convolve_kernel(
    group, lead_ref, inv_ref, trail_ref, back_ref, twist_ref, signal_ref, filter_ref, out_ref,
    high, low,
):
    sources, _, _, _, local, _ = signal_ref.shape
    rows = sources * local
    lead, inv, twist = lead_ref[...], inv_ref[...], (twist_ref[0], twist_ref[1])
    for index in range(group):
        pair = jnp.concatenate(
            [signal_ref[:, 0, index, side].reshape(rows, LANES) for side in range(2)], 1
        )
        for side, value in enumerate(lead_stage(lead, twist, pair)):
            place = slice((2 * index + side) * rows, (2 * index + side + 1) * rows)
            high[place, :], low[place, :] = split(value)
    spectra = trail_stage(high[...], low[...], trail_ref)
    for index in range(group):
        fre, fim = filter_ref[index, :, :LANES], filter_ref[index, :, LANES:]
        for side in range(2):
            place = slice((2 * index + side) * rows, (2 * index + side + 1) * rows)
            re, im = spectra[place, :LANES], spectra[place, LANES:]
            if side == 0:
                product = jnp.concatenate([re * fre - im * fim, re * fim + im * fre], 1)
            else:
                product = jnp.concatenate([re * fre + im * fim, im * fre - re * fim], 1)
            high[place, :], low[place, :] = split(product)
    spectra = trail_stage(high[...], low[...], back_ref)
    for index in range(group):
        reals, imags = [], []
        for side in range(2):
            place = slice((2 * index + side) * rows, (2 * index + side + 1) * rows)
            re, im = spectra[place, :LANES], spectra[place, LANES:]
            reals.append(re * twist[0] + im * twist[1])
            imags.append(im * twist[0] - re * twist[1])
        turned = jnp.concatenate([jnp.concatenate(reals, 1), jnp.concatenate(imags, 1)], 0)
        top, rest = split(turned)
        both = dot(inv, top)
        result = both[:rows] + both[rows:] + dot(inv[:rows], rest)
        result = result.astype(bf16)
        for side in range(2):
            lanes = slice(side * LANES, (side + 1) * LANES)
            out_ref[:, index, side] = result[:, lanes].reshape(sources, local, LANES)


def convolve(signals, spectrum, tables, which, place, group):
    lead_fwd, lead_inv, trail_fwd, trail_inv, twist = tables
    sources, _, inner, _, local, _ = signals.shape
    rows = sources * local
    whole = lambda ndim: (lambda *_: (0,) * ndim)
    return pl.pallas_call(
        functools.partial(convolve_kernel, group),
        out_shape=jax.ShapeDtypeStruct((sources, inner, 2, local, LANES), bf16),
        grid=(inner // group,),
        in_specs=[
            pl.BlockSpec(lead_fwd.shape, whole(2)),
            pl.BlockSpec(lead_inv.shape, whole(2)),
            pl.BlockSpec(trail_fwd.shape, whole(3)),
            pl.BlockSpec(trail_inv.shape, whole(3)),
            pl.BlockSpec(twist.shape, whole(3)),
            pl.BlockSpec(
                (sources, 1, group, 2, local, LANES), lambda step: (0, which, step, 0, 0, 0)
            ),
            pl.BlockSpec(
                (group, rows, 2 * LANES), lambda step: (place // group + step, 0, 0)
            ),
        ],
        out_specs=pl.BlockSpec((sources, group, 2, local, LANES), lambda step: (0, step, 0, 0, 0)),
        scratch_shapes=[pltpu.VMEM((2 * group * rows, 2 * LANES), bf16)] * 2,
        compiler_params=pltpu.CompilerParams(vmem_limit_bytes=VMEM_BYTES),
        cost_estimate=pl.CostEstimate(
            flops=inner * 10**6, bytes_accessed=2**20, transcendentals=0
        ),
        name="convolve",
    )(lead_fwd, lead_inv, trail_fwd, trail_inv, twist, signals, spectrum)


def gate_kernel(key_ref, value_ref, query_ref, grad_ref, out_ref, scratch):
    tokens, width = key_ref.shape
    local = tokens // LANES
    pitch = scratch.shape[0] // local
    dests, _, inner, _, _, _ = out_ref.shape
    for side, (one, two) in enumerate(((key_ref, value_ref), (grad_ref, query_ref))):
        for row in range(local):
            place = slice(row * LANES, (row + 1) * LANES)
            product = one[place, :].astype(f32) * two[place, :].astype(f32)
            scratch[row * pitch : row * pitch + width, :] = product.T
        for dest in range(dests):
            for index in range(inner):
                column = dest * inner + index
                out_ref[dest, 0, index, side] = scratch[
                    pl.ds(column, local, stride=pitch), :
                ].astype(bf16)


def gate(key_proj, value_proj, query_proj, out_grad, first, parts, groups, inner):
    tokens = key_proj.shape[0]
    local = tokens // LANES
    dests = LANES // inner
    blocks = groups // dests
    column = pl.BlockSpec((tokens, LANES), lambda step: (0, first * blocks + step))
    return pl.pallas_call(
        gate_kernel,
        out_shape=jax.ShapeDtypeStruct((groups, parts, inner, 2, local, LANES), bf16),
        grid=(parts * blocks,),
        in_specs=[column] * 4,
        out_specs=pl.BlockSpec(
            (dests, 1, inner, 2, local, LANES),
            lambda step: (step % blocks, step // blocks, 0, 0, 0, 0),
        ),
        scratch_shapes=[pltpu.VMEM((local * (LANES + 8), LANES), f32)],
        compiler_params=pltpu.CompilerParams(vmem_limit_bytes=VMEM_BYTES),
        cost_estimate=pl.CostEstimate(
            flops=0, bytes_accessed=2**20, transcendentals=0
        ),
        name="gate",
    )(key_proj, value_proj, query_proj, out_grad)


def finish_kernel(skip_ref, conv_ref, key_ref, value_ref, query_ref, grad_ref, *refs):
    out_ref, query_out, key_out, value_out, scratch = refs[-5:]
    tokens, width = key_ref.shape
    local = tokens // LANES
    dests, inner = conv_ref.shape[:2]
    skip = skip_ref[...]
    for side in range(2):
        for dest in range(dests):
            for index in range(inner):
                row = (dest * inner + index) * local
                scratch[side, row : row + local, :] = conv_ref[dest, index, side].astype(f32)
    for row in range(local):
        place = slice(row * LANES, (row + 1) * LANES)
        key, value = key_ref[place, :].astype(f32), value_ref[place, :].astype(f32)
        query, grad = query_ref[place, :].astype(f32), grad_ref[place, :].astype(f32)
        convolved = scratch[0, pl.ds(row, width, stride=local), :].T
        reflected = scratch[1, pl.ds(row, width, stride=local), :].T
        summed = convolved + skip * (key * value).astype(bf16).astype(f32)
        grad_sum = reflected + skip * (grad * query).astype(bf16).astype(f32)
        out_ref[place, :] = (query * summed).astype(bf16)
        query_out[place, :] = (grad * summed).astype(bf16)
        key_out[place, :] = (grad_sum * value).astype(bf16)
        value_out[place, :] = (grad_sum * key).astype(bf16)


def finish(skip, conv, key_proj, value_proj, query_proj, out_grad, part, previous):
    groups, inner = conv.shape[:2]
    tokens = key_proj.shape[0]
    dests = LANES // inner
    blocks = groups // dests
    local = tokens // LANES
    column = pl.BlockSpec((tokens, LANES), lambda step: (0, part * blocks + step))
    keep = [pl.BlockSpec(memory_space=pl.ANY)] * len(previous)
    return pl.pallas_call(
        finish_kernel,
        out_shape=[jax.ShapeDtypeStruct(key_proj.shape, bf16)] * 4,
        grid=(blocks,),
        in_specs=[
            pl.BlockSpec((1, LANES), lambda step: (0, part * blocks + step)),
            pl.BlockSpec((dests, inner, 2, local, LANES), lambda step: (step, 0, 0, 0, 0)),
        ]
        + [column] * 4
        + keep,
        out_specs=[column] * 4,
        scratch_shapes=[pltpu.VMEM((2, LANES * local, LANES), f32)],
        input_output_aliases={6 + index: index for index in range(len(previous))},
        compiler_params=pltpu.CompilerParams(vmem_limit_bytes=VMEM_BYTES),
        cost_estimate=pl.CostEstimate(
            flops=0, bytes_accessed=2**20, transcendentals=0
        ),
        name="finish",
    )(skip, conv, key_proj, value_proj, query_proj, out_grad, *previous)


def swap(value, axis="ctx"):
    return lax.all_to_all(value, axis, split_axis=0, concat_axis=0, tiled=True)


def fast_shards(query_proj, key_proj, value_proj, out_grad, long_filter, skip_gain, parts, halves):
    groups, planes = lax.axis_size("ctx"), lax.axis_size("ch")
    tokens, width = key_proj.shape
    channels, taps = long_filter.shape
    rows = groups * tokens // LANES
    inner = width // (groups * parts)
    tables = make_tables(rows)
    lead_fwd, lead_inv, trail_fwd, trail_inv, twist = (jnp.asarray(table) for table in tables)
    tables = (lead_fwd, lead_inv, trail_fwd, trail_inv, twist)
    plane = lax.axis_index("ch")

    sent = long_filter.reshape(planes, parts, groups, inner, taps).transpose(2, 0, 1, 3, 4)
    taken = swap(sent)
    per_half = parts // halves

    tiles = taps // LANES
    order = lead_fwd.reshape(2 * rows, 2, planes, groups, tiles).transpose(0, 1, 4, 2, 3)
    index = jnp.arange(planes) ^ plane
    lead_taps = jnp.take(order, index, axis=3).reshape(lead_fwd.shape)

    def pieces_of(taken, half):
        cut = taken[:, :, half * per_half : (half + 1) * per_half]
        found = []
        for step in range(planes):
            piece = lax.dynamic_index_in_dim(cut, plane ^ step, 1, keepdims=False)
            if step:
                piece = lax.ppermute(piece, "ch", [(i, i ^ step) for i in range(planes)])
            found.append(piece)
        return found

    outputs = []
    skip = skip_gain.reshape(1, width)
    signals = []
    gates = [
        gate(key_proj, value_proj, query_proj, out_grad, half * per_half, per_half, groups, inner)
        for half in range(halves)
    ]
    pieces = []
    for half in range(halves):
        before = (taken, signals[-1], pieces[-1]) if half else taken
        gates[half], before = lax.optimization_barrier((gates[half], before))
        taken = before[0] if half else before
        signals.append(swap(gates[half]))
        pieces.append(pieces_of(taken, half))
    for half in range(halves):
        spectra = filter_spectrum(pieces[half], lead_taps, trail_fwd, twist, TILE)
        for part in range(per_half):
            conv = convolve(signals[half], spectra, tables, part, part * inner, 16)
            if half < halves - 1:
                conv, pieces[half + 1], signals[half + 1] = lax.optimization_barrier(
                    (conv, pieces[half + 1], signals[half + 1])
                )
            outputs = finish(
                skip, swap(conv), key_proj, value_proj, query_proj, out_grad,
                half * per_half + part, outputs,
            )
    return tuple(outputs)


def plain_shards(query_proj, key_proj, value_proj, out_grad, long_filter, skip_gain):
    groups, planes = lax.axis_size("ctx"), lax.axis_size("ch")
    tokens, width = key_proj.shape
    channels, taps = long_filter.shape
    inner = width // groups
    length = groups * tokens
    rows = length // LANES
    tables = tuple(jnp.asarray(table) for table in make_tables(rows))
    group = 2 if inner % 2 == 0 else 1
    sent = long_filter.reshape(planes, groups, inner, taps).transpose(1, 0, 2, 3)
    taken = swap(swap(sent).transpose(1, 0, 2, 3), "ch")
    filters = taken.transpose(2, 0, 1, 3).reshape(inner, rows, LANES)
    lead, twist = tables[0].astype(f32), tables[4]
    lead = lead[:, :rows] + lead[:, rows:]
    trail = tables[2].astype(f32)
    highest = lax.Precision.HIGHEST
    turned = jnp.einsum("kn,cnm->ckm", lead, filters.astype(f32), precision=highest)
    real, imag = turned[:, :rows], turned[:, rows:]
    turned = jnp.concatenate(
        [real * twist[0] - imag * twist[1], real * twist[1] + imag * twist[0]], 2
    )
    spectrum = jnp.einsum("ckm,mj->ckj", turned, trail[0] + trail[1], precision=highest)
    gated_kv = (key_proj.astype(f32) * value_proj.astype(f32)).astype(bf16)
    grad_gate = (out_grad.astype(f32) * query_proj.astype(f32)).astype(bf16)
    both = jnp.stack([gated_kv.T, grad_gate.T], 1)
    taken = swap(both.reshape(groups, inner, 2, tokens))
    signals = taken.transpose(1, 2, 0, 3).reshape(1, 1, inner, 2, rows, LANES)
    conv = convolve(signals, spectrum, tables, 0, 0, group)
    back = conv.reshape(inner, 2, groups, tokens).transpose(2, 0, 1, 3)
    back = swap(back).reshape(width, 2, tokens)
    convolved, reflected = back[:, 0].T, back[:, 1].T
    summed = convolved.astype(f32) + skip_gain[None, :] * gated_kv.astype(f32)
    grad_sum = reflected.astype(f32) + skip_gain[None, :] * grad_gate.astype(f32)
    return (
        (query_proj.astype(f32) * summed).astype(bf16),
        (out_grad.astype(f32) * summed).astype(bf16),
        (grad_sum * value_proj.astype(f32)).astype(bf16),
        (grad_sum * key_proj.astype(f32)).astype(bf16),
    )


def shards(query_proj, key_proj, value_proj, out_grad, long_filter, skip_gain):
    groups = lax.axis_size("ctx")
    tokens, width = key_proj.shape
    planes = lax.axis_size("ch")
    taps = long_filter.shape[1]
    args = (query_proj, key_proj, value_proj, out_grad, long_filter, skip_gain)
    parts = 2
    inner = width // (groups * parts)
    fits = (
        tokens % (TILE * LANES) == 0
        and taps % LANES == 0
        and width % (groups * parts) == 0
        and inner % TILE == 0
        and LANES % inner == 0
        and groups % (LANES // inner) == 0
        and planes & (planes - 1) == 0
    )
    if fits:
        return fast_shards(*args, parts, 2)
    return plain_shards(*args)


def solution(mesh):
    placed = (
        P("ctx", "ch"),
        P("ctx", "ch"),
        P("ctx", "ch"),
        P("ctx", "ch"),
        P(None, ("ch", "ctx")),
        P("ch"),
    )
    return jax.shard_map(
        shards,
        mesh=mesh,
        in_specs=placed,
        out_specs=(P("ctx", "ch"), P("ctx", "ch"), P("ctx", "ch"), P("ctx", "ch")),
        check_vma=False,
    )
```

```python
import functools
import math

import jax
import jax.numpy as jnp
import ml_dtypes
import numpy as np
from jax import lax
from jax.experimental import pallas as pl
from jax.experimental.pallas import tpu as pltpu
from jax.sharding import PartitionSpec as P

LANES = 128
TILE = 16
VMEM_BYTES = 56 * 1024 * 1024

f32 = jnp.float32
bf16 = jnp.bfloat16


def two_parts(matrix):
    high = matrix.astype(ml_dtypes.bfloat16)
    low = (matrix - high.astype(np.float64)).astype(ml_dtypes.bfloat16)
    return high, low


def make_tables(rows):
    points = rows * LANES
    n1, k1 = np.arange(rows), np.arange(rows)
    n2, k2 = np.arange(LANES), np.arange(LANES)
    lead = 2 * math.pi / rows * np.outer(k1 + 0.25, n1)
    twist = 2 * math.pi / points * np.outer(k1 + 0.25, n2)
    trail = 2 * math.pi / LANES * np.outer(n2, k2)
    lead_fwd = np.concatenate([np.cos(lead), -np.sin(lead)], 0)
    lead_inv = np.concatenate([np.cos(lead).T, -np.sin(lead).T], 1) / points
    cosine, sine = np.cos(trail), np.sin(trail)
    trail_fwd = np.block([[cosine, -sine], [sine, cosine]])
    trail_inv = np.block([[cosine, sine], [-sine, cosine]])
    lead_fwd = np.concatenate(two_parts(lead_fwd), 1)
    lead_inv = np.concatenate(two_parts(lead_inv), 0)
    high, low = two_parts(trail_fwd)
    trail_fwd = np.concatenate([high, high, low], 0)
    high, low = two_parts(trail_inv)
    trail_inv = np.concatenate([high, high, low], 0)
    twist = np.stack([np.cos(twist), -np.sin(twist)]).astype(np.float32)
    return lead_fwd, lead_inv, trail_fwd, trail_inv, twist


def dot(left, right):
    return jnp.dot(left, right, preferred_element_type=f32)


def split(value):
    high = value.astype(bf16)
    return high, (value - high.astype(f32)).astype(bf16)


def lead_stage(lead, twist, pair):
    rows = pair.shape[0]
    turned = dot(lead, jnp.concatenate([pair, pair], 0))
    real, imag = turned[:rows], turned[rows:]
    parts = []
    for side in range(2):
        lanes = slice(side * LANES, (side + 1) * LANES)
        re, im = real[:, lanes], imag[:, lanes]
        parts.append(
            jnp.concatenate([re * twist[0] - im * twist[1], re * twist[1] + im * twist[0]], 1)
        )
    return parts


def store_split(ref, place, value):
    high, low = split(value)
    width = value.shape[1]
    ref[place, :width] = high
    ref[place, width : 2 * width] = low
    ref[place, 2 * width :] = high


def spectrum_kernel(pieces, group, lead_ref, trail_ref, twist_ref, *refs):
    taps = refs[:pieces]
    out_ref, scratch, wide = refs[pieces:]
    sources, _, _, width = taps[0].shape
    count = pieces * sources
    for piece in range(pieces):
        for source in range(sources):
            row = (piece * sources + source) * group
            for part in range(width // LANES):
                lanes = slice(part * LANES, (part + 1) * LANES)
                scratch[part, row : row + group, :] = taps[piece][source, 0, :, lanes].astype(f32)
    lead, twist = lead_ref[...], (twist_ref[0], twist_ref[1])
    rows = count * (width // LANES)

    def channel(index):
        parts = [
            scratch[part, pl.ds(index, count, stride=group), :] for part in range(width // LANES)
        ]
        return jnp.concatenate(parts, 0).astype(bf16)

    for index in range(0, group, 2):
        pair = jnp.concatenate([channel(index), channel(index + 1)], 1)
        for side, value in enumerate(lead_stage(lead, twist, pair)):
            place = slice((index + side) * rows, (index + side + 1) * rows)
            store_split(wide, place, value)
    step = 4
    for index in range(0, group, step):
        product = dot(wide[index * rows : (index + step) * rows, :], trail_ref[...])
        out_ref[index : index + step] = product.reshape(step, rows, 2 * LANES)


def filter_spectrum(pieces, lead, trail, twist, group):
    sources, outer, inner, width = pieces[0].shape
    rows = lead.shape[1] // 2
    steps = inner // group
    whole = lambda ndim: (lambda *_: (0,) * ndim)
    return pl.pallas_call(
        functools.partial(spectrum_kernel, len(pieces), group),
        out_shape=jax.ShapeDtypeStruct((outer * inner, rows, 2 * LANES), f32),
        grid=(outer * steps,),
        in_specs=[
            pl.BlockSpec(lead.shape, whole(2)),
            pl.BlockSpec(trail.shape, whole(2)),
            pl.BlockSpec(twist.shape, whole(3)),
        ]
        + [
            pl.BlockSpec(
                (sources, 1, group, width), lambda step: (0, step // steps, step % steps, 0)
            )
        ]
        * len(pieces),
        out_specs=pl.BlockSpec((group, rows, 2 * LANES), lambda step: (step, 0, 0)),
        scratch_shapes=[
            pltpu.VMEM((width // LANES, len(pieces) * sources * group, LANES), f32),
            pltpu.VMEM((group * rows, 6 * LANES), bf16),
        ],
        compiler_params=pltpu.CompilerParams(vmem_limit_bytes=VMEM_BYTES),
        cost_estimate=pl.CostEstimate(
            flops=outer * inner * 10**6, bytes_accessed=2**20, transcendentals=0
        ),
        name="filter_spectrum",
    )(lead, trail, twist, *pieces)


def convolve_kernel(
    group, sources, lead_ref, inv_ref, trail_ref, back_ref, twist_ref, filter_ref, *refs
):
    signals, outs, (wide, spectra) = refs[:sources], refs[sources:-2], refs[-2:]
    local = signals[0].shape[2]
    rows = sources * local
    lead, inv, twist = lead_ref[...], inv_ref[...], (twist_ref[0], twist_ref[1])
    for index in range(group):
        pair = jnp.concatenate(
            [jnp.concatenate([ref[index, side] for ref in signals], 0) for side in range(2)], 1
        )
        for side, value in enumerate(lead_stage(lead, twist, pair)):
            place = slice((2 * index + side) * rows, (2 * index + side + 1) * rows)
            store_split(wide, place, value)
    for row in range(0, wide.shape[0], 512):
        spectra[row : row + 512, :] = dot(wide[row : row + 512, :], trail_ref[...])
    for index in range(group):
        fre, fim = filter_ref[index, :, :LANES], filter_ref[index, :, LANES:]
        for side in range(2):
            place = slice((2 * index + side) * rows, (2 * index + side + 1) * rows)
            re, im = spectra[place, :LANES], spectra[place, LANES:]
            if side == 0:
                product = jnp.concatenate([re * fre - im * fim, re * fim + im * fre], 1)
            else:
                product = jnp.concatenate([re * fre + im * fim, im * fre - re * fim], 1)
            store_split(wide, place, product)
    for row in range(0, wide.shape[0], 512):
        spectra[row : row + 512, :] = dot(wide[row : row + 512, :], back_ref[...])
    for index in range(group):
        reals, imags = [], []
        for side in range(2):
            place = slice((2 * index + side) * rows, (2 * index + side + 1) * rows)
            re, im = spectra[place, :LANES], spectra[place, LANES:]
            reals.append(re * twist[0] + im * twist[1])
            imags.append(im * twist[0] - re * twist[1])
        turned = jnp.concatenate([jnp.concatenate(reals, 1), jnp.concatenate(imags, 1)], 0)
        top, rest = split(turned)
        both = dot(inv, top)
        result = both[:rows] + both[rows:] + dot(inv[:rows], rest)
        result = result.astype(bf16)
        for side in range(2):
            lanes = slice(side * LANES, (side + 1) * LANES)
            for source in range(sources):
                value = result[source * local : (source + 1) * local, lanes]
                if len(outs[0].shape) == 5:
                    outs[0][source, index, side] = value
                else:
                    outs[source][index, side] = value


def convolve(signals, spectrum, tables, group, whole_out=False):
    lead_fwd, lead_inv, trail_fwd, trail_inv, twist = tables
    sources = len(signals)
    inner, _, local, _ = signals[0].shape
    rows = sources * local
    whole = lambda ndim: (lambda *_: (0,) * ndim)
    piece = pl.BlockSpec((group, 2, local, LANES), lambda step: (step, 0, 0, 0))
    if whole_out:
        out_shape = [jax.ShapeDtypeStruct((sources, inner, 2, local, LANES), bf16)]
        out_specs = [
            pl.BlockSpec((sources, group, 2, local, LANES), lambda step: (0, step, 0, 0, 0))
        ]
    else:
        out_shape = [jax.ShapeDtypeStruct((inner, 2, local, LANES), bf16)] * sources
        out_specs = [piece] * sources
    return pl.pallas_call(
        functools.partial(convolve_kernel, group, sources),
        out_shape=out_shape,
        grid=(inner // group,),
        in_specs=[
            pl.BlockSpec(lead_fwd.shape, whole(2)),
            pl.BlockSpec(lead_inv.shape, whole(2)),
            pl.BlockSpec(trail_fwd.shape, whole(2)),
            pl.BlockSpec(trail_inv.shape, whole(2)),
            pl.BlockSpec(twist.shape, whole(3)),
            pl.BlockSpec((group, rows, 2 * LANES), lambda step: (step, 0, 0)),
        ]
        + [piece] * sources,
        out_specs=out_specs,
        scratch_shapes=[
            pltpu.VMEM((2 * group * rows, 6 * LANES), bf16),
            pltpu.VMEM((2 * group * rows, 2 * LANES), f32),
        ],
        compiler_params=pltpu.CompilerParams(vmem_limit_bytes=VMEM_BYTES),
        cost_estimate=pl.CostEstimate(
            flops=inner * 10**6, bytes_accessed=2**20, transcendentals=0
        ),
        name="convolve",
    )(lead_fwd, lead_inv, trail_fwd, trail_inv, twist, spectrum, *signals)


def gate_kernel(me_ref, key_ref, value_ref, query_ref, grad_ref, *refs):
    outs, scratch = refs[:-1], refs[-1]
    tokens, width = key_ref.shape
    local = tokens // LANES
    pitch = scratch.shape[1] // local
    inner = outs[0].shape[0]
    dests = width // inner
    mine = lax.rem(me_ref[0], dests)
    for side, (one, two) in enumerate(((key_ref, value_ref), (grad_ref, query_ref))):
        for row in range(local):
            place = slice(row * LANES, (row + 1) * LANES)
            product = one[place, :].astype(f32) * two[place, :].astype(f32)
            scratch[side, row * pitch : row * pitch + width, :] = product.T
    for block in range(len(outs) // dests):

        @pl.when(pl.program_id(0) == block)
        def _():
            for slot in range(dests):
                base = (mine ^ slot) * inner
                for side in range(2):
                    for index in range(inner):
                        outs[block * dests + slot][index, side] = scratch[
                            side, pl.ds(base + index, local, stride=pitch), :
                        ].astype(bf16)


def gate(me, key_proj, value_proj, query_proj, out_grad, part, groups, inner):
    tokens = key_proj.shape[0]
    local = tokens // LANES
    dests = LANES // inner
    blocks = groups // dests
    column = pl.BlockSpec(
        (tokens, LANES), lambda step, me: (0, part * blocks + ((me[0] // dests) ^ step))
    )
    piece = (inner, 2, local, LANES)
    return pl.pallas_call(
        gate_kernel,
        out_shape=[jax.ShapeDtypeStruct(piece, bf16)] * groups,
        grid_spec=pltpu.PrefetchScalarGridSpec(
            num_scalar_prefetch=1,
            grid=(blocks,),
            in_specs=[column] * 4,
            out_specs=[pl.BlockSpec(piece, lambda step, me: (0, 0, 0, 0))] * groups,
            scratch_shapes=[pltpu.VMEM((2, local * (LANES + 8), LANES), f32)],
        ),
        compiler_params=pltpu.CompilerParams(vmem_limit_bytes=VMEM_BYTES),
        cost_estimate=pl.CostEstimate(flops=0, bytes_accessed=2**20, transcendentals=0),
        name="gate",
    )(me, key_proj, value_proj, query_proj, out_grad)


def finish_kernel(pieces_count, me_ref, skip_ref, key_ref, value_ref, query_ref, grad_ref, *refs):
    pieces = refs[:pieces_count]
    out_ref, query_out, key_out, value_out, scratch = refs[-5:]
    tokens, width = key_ref.shape
    local = tokens // LANES
    pitch = scratch.shape[1] // width
    inner = pieces[0].shape[-4]
    dests = width // inner
    mine = lax.rem(me_ref[0], dests)
    skip = skip_ref[...]
    if pieces_count == 1:
        for slot in range(dests):
            for side in range(2):
                for index in range(inner):
                    row = (slot * inner + index) * pitch
                    scratch[side, row : row + local, :] = pieces[0][slot, index, side].astype(f32)
    for block in range(pieces_count // dests):

        @pl.when(pl.program_id(0) == block)
        def _():
            for slot in range(dests):
                base = (mine ^ slot) * (inner * pitch)
                for side in range(2):
                    for index in range(inner):
                        scratch[side, pl.ds(base + index * pitch, local), :] = pieces[
                            block * dests + slot
                        ][index, side].astype(f32)

    for row in range(local):
        place = slice(row * LANES, (row + 1) * LANES)
        key, value = key_ref[place, :].astype(f32), value_ref[place, :].astype(f32)
        query, grad = query_ref[place, :].astype(f32), grad_ref[place, :].astype(f32)
        convolved = scratch[0, pl.ds(row, width, stride=pitch), :].T
        reflected = scratch[1, pl.ds(row, width, stride=pitch), :].T
        summed = convolved + skip * (key * value).astype(bf16).astype(f32)
        grad_sum = reflected + skip * (grad * query).astype(bf16).astype(f32)
        out_ref[place, :] = (query * summed).astype(bf16)
        query_out[place, :] = (grad * summed).astype(bf16)
        key_out[place, :] = (grad_sum * value).astype(bf16)
        value_out[place, :] = (grad_sum * key).astype(bf16)


def finish(me, skip, pieces, key_proj, value_proj, query_proj, out_grad, part, groups, previous):
    inner, _, local, _ = pieces[0].shape[-4:]
    tokens = key_proj.shape[0]
    dests = LANES // inner
    blocks = groups // dests
    whole = len(pieces) == 1

    def place(step, me):
        return 0, part * blocks + (step if whole else (me[0] // dests) ^ step)

    column = pl.BlockSpec((tokens, LANES), place)
    if whole:
        piece = pl.BlockSpec((dests, inner, 2, local, LANES), lambda step, me: (step, 0, 0, 0, 0))
    else:
        piece = pl.BlockSpec(pieces[0].shape, lambda step, me: (0, 0, 0, 0))
    return pl.pallas_call(
        functools.partial(finish_kernel, len(pieces)),
        out_shape=[jax.ShapeDtypeStruct(key_proj.shape, bf16)] * 4,
        grid_spec=pltpu.PrefetchScalarGridSpec(
            num_scalar_prefetch=1,
            grid=(blocks,),
            in_specs=[pl.BlockSpec((1, LANES), place)]
            + [column] * 4
            + [piece] * len(pieces)
            + [pl.BlockSpec(memory_space=pl.ANY)] * len(previous),
            out_specs=[column] * 4,
            scratch_shapes=[pltpu.VMEM((2, LANES * (local + 1), LANES), f32)],
        ),
        input_output_aliases={6 + len(pieces) + index: index for index in range(len(previous))},
        compiler_params=pltpu.CompilerParams(vmem_limit_bytes=VMEM_BYTES),
        cost_estimate=pl.CostEstimate(flops=0, bytes_accessed=2**20, transcendentals=0),
        name="finish",
    )(me, skip, key_proj, value_proj, query_proj, out_grad, *pieces, *previous)


def swap(value, axis="ctx"):
    return lax.all_to_all(value, axis, split_axis=0, concat_axis=0, tiled=True)


def tie(values, *others):
    return lax.optimization_barrier((values, others))[0]


def exchange(pieces, axis, order=None):
    count = len(pieces)
    taken = list(pieces)
    for step in order or range(1, count):
        taken[step] = lax.ppermute(pieces[step], axis, [(i, i ^ step) for i in range(count)])
    return taken


def fast_shards(query_proj, key_proj, value_proj, out_grad, long_filter, skip_gain, parts):
    groups, planes = lax.axis_size("ctx"), lax.axis_size("ch")
    tokens, width = key_proj.shape
    channels, taps = long_filter.shape
    rows = groups * tokens // LANES
    local, tiles = tokens // LANES, taps // LANES
    inner = width // (groups * parts)
    tables = make_tables(rows)
    lead_taps = tables[0].reshape(2 * rows, 2, planes * groups, tiles).transpose(0, 1, 3, 2)
    lead_taps = jnp.asarray(lead_taps.reshape(2 * rows, 2 * rows))
    lead_fwd, lead_inv, trail_fwd, trail_inv, twist = (jnp.asarray(table) for table in tables)
    me = lax.axis_index("ctx")
    place = jnp.full((1,), me, jnp.int32)

    sources = jnp.arange(groups) ^ me
    lead = jnp.take(lead_fwd.reshape(2 * rows, 2, groups, local), sources, axis=2)
    lead = lead.reshape(lead_fwd.shape)
    back = jnp.take(lead_inv.reshape(2, groups, local, 2 * rows), sources, axis=1)
    back = back.reshape(lead_inv.shape)

    skip = skip_gain.reshape(1, width)
    shaped = long_filter.reshape(planes, parts, groups, inner, taps)
    gates = [
        gate(place, key_proj, value_proj, query_proj, out_grad, part, groups, inner)
        for part in range(parts)
    ]
    late = (1,)

    slabs = [shaped[:, 0]] + [tie(shaped, gates[0])[:, part] for part in range(1, parts)]

    def send_filter(part, *others):
        slab = slabs[part].reshape(planes * groups, inner, taps)
        return swap(tie(slab, *others), ("ch", "ctx"))

    filters = send_filter(0)
    signals = exchange(gates[0], "ctx")
    outputs = []
    for part in range(parts):
        last = part == parts - 1
        if not last:
            following = send_filter(part + 1, filters, signals, gates[part + 1])
            early = [step for step in range(groups) if step not in late]
            pieces = tie(gates[part + 1], filters, signals)
            coming = exchange(pieces, "ctx", early)
        spectrum = filter_spectrum([filters[:, None]], lead_taps, trail_fwd, twist, TILE)
        tables = (lead, back if last else lead_inv, trail_fwd, trail_inv, twist)
        conv = convolve(signals, spectrum, tables, TILE, not last)
        if last:
            taken = exchange(conv, "ctx")
        else:
            for step in late:
                coming[step] = tie(pieces[step], conv[0])
            rest = exchange(coming, "ctx", late)
            coming = [rest[step] if step in late else coming[step] for step in range(groups)]
            conv, following, coming = lax.optimization_barrier((conv[0], following, coming))
            taken = [swap(conv)]
            filters, signals = following, coming
        outputs = finish(
            place, skip, taken, key_proj, value_proj, query_proj, out_grad, part, groups, outputs
        )
    return tuple(outputs)


def plain_shards(query_proj, key_proj, value_proj, out_grad, long_filter, skip_gain):
    groups, planes = lax.axis_size("ctx"), lax.axis_size("ch")
    tokens, width = key_proj.shape
    channels, taps = long_filter.shape
    inner = width // groups
    length = groups * tokens
    rows = length // LANES
    tables = tuple(jnp.asarray(table) for table in make_tables(rows))
    group = 2 if inner % 2 == 0 else 1
    sent = long_filter.reshape(planes, groups, inner, taps).transpose(1, 0, 2, 3)
    taken = swap(swap(sent).transpose(1, 0, 2, 3), "ch")
    filters = taken.transpose(2, 0, 1, 3).reshape(inner, rows, LANES)
    lead, twist = tables[0].astype(f32), tables[4]
    lead = lead[:, :rows] + lead[:, rows:]
    trail = tables[2].astype(f32)[2 * LANES :]
    trail = trail[: 2 * LANES] + trail[2 * LANES :]
    highest = lax.Precision.HIGHEST
    turned = jnp.einsum("kn,cnm->ckm", lead, filters.astype(f32), precision=highest)
    real, imag = turned[:, :rows], turned[:, rows:]
    turned = jnp.concatenate(
        [real * twist[0] - imag * twist[1], real * twist[1] + imag * twist[0]], 2
    )
    spectrum = jnp.einsum("ckm,mj->ckj", turned, trail, precision=highest)
    gated_kv = (key_proj.astype(f32) * value_proj.astype(f32)).astype(bf16)
    grad_gate = (out_grad.astype(f32) * query_proj.astype(f32)).astype(bf16)
    both = jnp.stack([gated_kv.T, grad_gate.T], 1)
    taken = swap(both.reshape(groups, inner, 2, tokens))
    signals = taken.transpose(1, 2, 0, 3).reshape(inner, 2, rows, LANES)
    (conv,) = convolve([signals], spectrum, tables, group)
    back = conv.reshape(inner, 2, groups, tokens).transpose(2, 0, 1, 3)
    back = swap(back).reshape(width, 2, tokens)
    convolved, reflected = back[:, 0].T, back[:, 1].T
    summed = convolved.astype(f32) + skip_gain[None, :] * gated_kv.astype(f32)
    grad_sum = reflected.astype(f32) + skip_gain[None, :] * grad_gate.astype(f32)
    return (
        (query_proj.astype(f32) * summed).astype(bf16),
        (out_grad.astype(f32) * summed).astype(bf16),
        (grad_sum * value_proj.astype(f32)).astype(bf16),
        (grad_sum * key_proj.astype(f32)).astype(bf16),
    )


def shards(query_proj, key_proj, value_proj, out_grad, long_filter, skip_gain):
    groups = lax.axis_size("ctx")
    tokens, width = key_proj.shape
    planes = lax.axis_size("ch")
    taps = long_filter.shape[1]
    args = (query_proj, key_proj, value_proj, out_grad, long_filter, skip_gain)
    parts = 2
    inner = width // (groups * parts)
    fits = (
        tokens % (TILE * LANES) == 0
        and taps % LANES == 0
        and width % (groups * parts) == 0
        and inner % TILE == 0
        and LANES % inner == 0
        and groups % (LANES // inner) == 0
        and planes & (planes - 1) == 0
        and groups & (groups - 1) == 0
    )
    if fits:
        return fast_shards(*args, parts)
    return plain_shards(*args)


def solution(mesh):
    placed = (
        P("ctx", "ch"),
        P("ctx", "ch"),
        P("ctx", "ch"),
        P("ctx", "ch"),
        P(None, ("ch", "ctx")),
        P("ch"),
    )
    return jax.shard_map(
        shards,
        mesh=mesh,
        in_specs=placed,
        out_specs=(P("ctx", "ch"), P("ctx", "ch"), P("ctx", "ch"), P("ctx", "ch")),
        check_vma=False,
    )
```

```python
import functools
import math

import jax
import jax.numpy as jnp
import ml_dtypes
import numpy as np
from jax import lax
from jax.experimental import pallas as pl
from jax.experimental.pallas import tpu as pltpu
from jax.sharding import PartitionSpec as P

LANES = 128
TILE = 16
VMEM_BYTES = 56 * 1024 * 1024

f32 = jnp.float32
bf16 = jnp.bfloat16


def two_parts(matrix):
    high = matrix.astype(ml_dtypes.bfloat16)
    low = (matrix - high.astype(np.float64)).astype(ml_dtypes.bfloat16)
    return high, low


def make_tables(rows):
    points = rows * LANES
    n1, k1 = np.arange(rows), np.arange(rows)
    n2, k2 = np.arange(LANES), np.arange(LANES)
    lead = 2 * math.pi / rows * np.outer(k1 + 0.25, n1)
    twist = 2 * math.pi / points * np.outer(k1 + 0.25, n2)
    trail = 2 * math.pi / LANES * np.outer(n2, k2)
    lead_fwd = np.concatenate([np.cos(lead), -np.sin(lead)], 0)
    lead_inv = np.concatenate([np.cos(lead).T, -np.sin(lead).T], 1) / points
    cosine, sine = np.cos(trail), np.sin(trail)
    trail_fwd = np.block([[cosine, -sine], [sine, cosine]])
    trail_inv = np.block([[cosine, sine], [-sine, cosine]])
    lead_fwd = np.concatenate(two_parts(lead_fwd), 1)
    lead_inv = np.concatenate(two_parts(lead_inv), 0)
    high, low = two_parts(trail_fwd)
    trail_fwd = np.concatenate([high, high, low], 0)
    high, low = two_parts(trail_inv)
    trail_inv = np.concatenate([high, high, low], 0)
    twist = np.stack([np.cos(twist), -np.sin(twist)]).astype(np.float32)
    return lead_fwd, lead_inv, trail_fwd, trail_inv, twist


def dot(left, right):
    return jnp.dot(left, right, preferred_element_type=f32)


def split(value):
    high = value.astype(bf16)
    return high, (value - high.astype(f32)).astype(bf16)


def lead_stage(lead, twist, pair):
    rows = pair.shape[0]
    turned = dot(lead, jnp.concatenate([pair, pair], 0))
    real, imag = turned[:rows], turned[rows:]
    parts = []
    for side in range(2):
        lanes = slice(side * LANES, (side + 1) * LANES)
        re, im = real[:, lanes], imag[:, lanes]
        parts.append(
            jnp.concatenate([re * twist[0] - im * twist[1], re * twist[1] + im * twist[0]], 1)
        )
    return parts


def store_split(ref, place, value):
    high, low = split(value)
    width = value.shape[1]
    ref[place, :width] = high
    ref[place, width : 2 * width] = low
    ref[place, 2 * width :] = high


def spectrum_kernel(pieces, group, lead_ref, trail_ref, twist_ref, *refs):
    taps = refs[:pieces]
    out_ref, scratch, wide = refs[pieces:]
    sources, _, _, width = taps[0].shape
    count = pieces * sources
    for piece in range(pieces):
        for source in range(sources):
            row = (piece * sources + source) * group
            for part in range(width // LANES):
                lanes = slice(part * LANES, (part + 1) * LANES)
                scratch[part, row : row + group, :] = taps[piece][source, 0, :, lanes].astype(f32)
    lead, twist = lead_ref[...], (twist_ref[0], twist_ref[1])
    rows = count * (width // LANES)

    def channel(index):
        parts = [
            scratch[part, pl.ds(index, count, stride=group), :] for part in range(width // LANES)
        ]
        return jnp.concatenate(parts, 0).astype(bf16)

    for index in range(0, group, 2):
        pair = jnp.concatenate([channel(index), channel(index + 1)], 1)
        for side, value in enumerate(lead_stage(lead, twist, pair)):
            place = slice((index + side) * rows, (index + side + 1) * rows)
            store_split(wide, place, value)
    step = 4
    for index in range(0, group, step):
        product = dot(wide[index * rows : (index + step) * rows, :], trail_ref[...])
        out_ref[index : index + step] = product.reshape(step, rows, 2 * LANES)


def filter_spectrum(pieces, lead, trail, twist, group):
    sources, outer, inner, width = pieces[0].shape
    rows = lead.shape[1] // 2
    steps = inner // group
    whole = lambda ndim: (lambda *_: (0,) * ndim)
    return pl.pallas_call(
        functools.partial(spectrum_kernel, len(pieces), group),
        out_shape=jax.ShapeDtypeStruct((outer * inner, rows, 2 * LANES), f32),
        grid=(outer * steps,),
        in_specs=[
            pl.BlockSpec(lead.shape, whole(2)),
            pl.BlockSpec(trail.shape, whole(2)),
            pl.BlockSpec(twist.shape, whole(3)),
        ]
        + [
            pl.BlockSpec(
                (sources, 1, group, width), lambda step: (0, step // steps, step % steps, 0)
            )
        ]
        * len(pieces),
        out_specs=pl.BlockSpec((group, rows, 2 * LANES), lambda step: (step, 0, 0)),
        scratch_shapes=[
            pltpu.VMEM((width // LANES, len(pieces) * sources * group, LANES), f32),
            pltpu.VMEM((group * rows, 6 * LANES), bf16),
        ],
        compiler_params=pltpu.CompilerParams(vmem_limit_bytes=VMEM_BYTES),
        cost_estimate=pl.CostEstimate(
            flops=outer * inner * 10**6, bytes_accessed=2**20, transcendentals=0
        ),
        name="filter_spectrum",
    )(lead, trail, twist, *pieces)


def convolve_kernel(
    group, sources, lead_ref, inv_ref, trail_ref, back_ref, twist_ref, filter_ref, *refs
):
    signals, outs, (wide, spectra) = refs[:sources], refs[sources:-2], refs[-2:]
    local = signals[0].shape[2]
    rows = sources * local
    lead, inv, twist = lead_ref[...], inv_ref[...], (twist_ref[0], twist_ref[1])
    for index in range(group):
        pair = jnp.concatenate(
            [jnp.concatenate([ref[index, side] for ref in signals], 0) for side in range(2)], 1
        )
        for side, value in enumerate(lead_stage(lead, twist, pair)):
            place = slice((2 * index + side) * rows, (2 * index + side + 1) * rows)
            store_split(wide, place, value)
    for row in range(0, wide.shape[0], 512):
        spectra[row : row + 512, :] = dot(wide[row : row + 512, :], trail_ref[...])
    for index in range(group):
        fre, fim = filter_ref[index, :, :LANES], filter_ref[index, :, LANES:]
        for side in range(2):
            place = slice((2 * index + side) * rows, (2 * index + side + 1) * rows)
            re, im = spectra[place, :LANES], spectra[place, LANES:]
            if side == 0:
                product = jnp.concatenate([re * fre - im * fim, re * fim + im * fre], 1)
            else:
                product = jnp.concatenate([re * fre + im * fim, im * fre - re * fim], 1)
            store_split(wide, place, product)
    for row in range(0, wide.shape[0], 512):
        spectra[row : row + 512, :] = dot(wide[row : row + 512, :], back_ref[...])
    for index in range(group):
        reals, imags = [], []
        for side in range(2):
            place = slice((2 * index + side) * rows, (2 * index + side + 1) * rows)
            re, im = spectra[place, :LANES], spectra[place, LANES:]
            reals.append(re * twist[0] + im * twist[1])
            imags.append(im * twist[0] - re * twist[1])
        turned = jnp.concatenate([jnp.concatenate(reals, 1), jnp.concatenate(imags, 1)], 0)
        top, rest = split(turned)
        both = dot(inv, top)
        result = both[:rows] + both[rows:] + dot(inv[:rows], rest)
        result = result.astype(bf16)
        for side in range(2):
            lanes = slice(side * LANES, (side + 1) * LANES)
            for source in range(sources):
                value = result[source * local : (source + 1) * local, lanes]
                if len(outs[0].shape) == 5:
                    outs[0][source, index, side] = value
                else:
                    outs[source][index, side] = value


def convolve(signals, spectrum, tables, group, whole_out=False):
    lead_fwd, lead_inv, trail_fwd, trail_inv, twist = tables
    sources = len(signals)
    inner, _, local, _ = signals[0].shape
    rows = sources * local
    whole = lambda ndim: (lambda *_: (0,) * ndim)
    piece = pl.BlockSpec((group, 2, local, LANES), lambda step: (step, 0, 0, 0))
    if whole_out:
        out_shape = [jax.ShapeDtypeStruct((sources, inner, 2, local, LANES), bf16)]
        out_specs = [
            pl.BlockSpec((sources, group, 2, local, LANES), lambda step: (0, step, 0, 0, 0))
        ]
    else:
        out_shape = [jax.ShapeDtypeStruct((inner, 2, local, LANES), bf16)] * sources
        out_specs = [piece] * sources
    return pl.pallas_call(
        functools.partial(convolve_kernel, group, sources),
        out_shape=out_shape,
        grid=(inner // group,),
        in_specs=[
            pl.BlockSpec(lead_fwd.shape, whole(2)),
            pl.BlockSpec(lead_inv.shape, whole(2)),
            pl.BlockSpec(trail_fwd.shape, whole(2)),
            pl.BlockSpec(trail_inv.shape, whole(2)),
            pl.BlockSpec(twist.shape, whole(3)),
            pl.BlockSpec((group, rows, 2 * LANES), lambda step: (step, 0, 0)),
        ]
        + [piece] * sources,
        out_specs=out_specs,
        scratch_shapes=[
            pltpu.VMEM((2 * group * rows, 6 * LANES), bf16),
            pltpu.VMEM((2 * group * rows, 2 * LANES), f32),
        ],
        compiler_params=pltpu.CompilerParams(vmem_limit_bytes=VMEM_BYTES),
        cost_estimate=pl.CostEstimate(
            flops=inner * 10**6, bytes_accessed=2**20, transcendentals=0
        ),
        name="convolve",
    )(lead_fwd, lead_inv, trail_fwd, trail_inv, twist, spectrum, *signals)


def gate_kernel(me_ref, key_ref, value_ref, query_ref, grad_ref, *refs):
    outs, scratch = refs[:-1], refs[-1]
    tokens, width = key_ref.shape
    local = tokens // LANES
    pitch = scratch.shape[1] // local
    inner = outs[0].shape[0]
    dests = width // inner
    mine = lax.rem(me_ref[0], dests)
    for side, (one, two) in enumerate(((key_ref, value_ref), (grad_ref, query_ref))):
        for row in range(local):
            place = slice(row * LANES, (row + 1) * LANES)
            product = one[place, :].astype(f32) * two[place, :].astype(f32)
            scratch[side, row * pitch : row * pitch + width, :] = product.T
    for block in range(len(outs) // dests):

        @pl.when(pl.program_id(0) == block)
        def _():
            for slot in range(dests):
                base = (mine ^ slot) * inner
                for side in range(2):
                    for index in range(inner):
                        outs[block * dests + slot][index, side] = scratch[
                            side, pl.ds(base + index, local, stride=pitch), :
                        ].astype(bf16)


def gate(me, key_proj, value_proj, query_proj, out_grad, part, groups, inner):
    tokens = key_proj.shape[0]
    local = tokens // LANES
    dests = LANES // inner
    blocks = groups // dests
    column = pl.BlockSpec(
        (tokens, LANES), lambda step, me: (0, part * blocks + ((me[0] // dests) ^ step))
    )
    piece = (inner, 2, local, LANES)
    return pl.pallas_call(
        gate_kernel,
        out_shape=[jax.ShapeDtypeStruct(piece, bf16)] * groups,
        grid_spec=pltpu.PrefetchScalarGridSpec(
            num_scalar_prefetch=1,
            grid=(blocks,),
            in_specs=[column] * 4,
            out_specs=[pl.BlockSpec(piece, lambda step, me: (0, 0, 0, 0))] * groups,
            scratch_shapes=[pltpu.VMEM((2, local * (LANES + 8), LANES), f32)],
        ),
        compiler_params=pltpu.CompilerParams(vmem_limit_bytes=VMEM_BYTES),
        cost_estimate=pl.CostEstimate(flops=0, bytes_accessed=2**20, transcendentals=0),
        name="gate",
    )(me, key_proj, value_proj, query_proj, out_grad)


def finish_kernel(pieces_count, me_ref, skip_ref, key_ref, value_ref, query_ref, grad_ref, *refs):
    pieces = refs[:pieces_count]
    out_ref, query_out, key_out, value_out, scratch = refs[-5:]
    tokens, width = key_ref.shape
    local = tokens // LANES
    pitch = scratch.shape[1] // width
    inner = pieces[0].shape[-4]
    dests = width // inner
    mine = lax.rem(me_ref[0], dests)
    skip = skip_ref[...]
    if pieces_count == 1:
        for slot in range(dests):
            for side in range(2):
                for index in range(inner):
                    row = (slot * inner + index) * pitch
                    scratch[side, row : row + local, :] = pieces[0][slot, index, side].astype(f32)
    for block in range(pieces_count // dests):

        @pl.when(pl.program_id(0) == block)
        def _():
            for slot in range(dests):
                base = (mine ^ slot) * (inner * pitch)
                for side in range(2):
                    for index in range(inner):
                        scratch[side, pl.ds(base + index * pitch, local), :] = pieces[
                            block * dests + slot
                        ][index, side].astype(f32)

    for row in range(local):
        place = slice(row * LANES, (row + 1) * LANES)
        key, value = key_ref[place, :].astype(f32), value_ref[place, :].astype(f32)
        query, grad = query_ref[place, :].astype(f32), grad_ref[place, :].astype(f32)
        convolved = scratch[0, pl.ds(row, width, stride=pitch), :].T
        reflected = scratch[1, pl.ds(row, width, stride=pitch), :].T
        summed = convolved + skip * (key * value).astype(bf16).astype(f32)
        grad_sum = reflected + skip * (grad * query).astype(bf16).astype(f32)
        out_ref[place, :] = (query * summed).astype(bf16)
        query_out[place, :] = (grad * summed).astype(bf16)
        key_out[place, :] = (grad_sum * value).astype(bf16)
        value_out[place, :] = (grad_sum * key).astype(bf16)


def finish(me, skip, pieces, spots, key_proj, value_proj, query_proj, out_grad, part, groups, previous):
    inner, _, local, _ = pieces[0].shape[-4:]
    tokens = key_proj.shape[0]
    dests = LANES // inner
    blocks = groups // dests
    whole = len(pieces) == 1
    if not whole:
        pieces = pieces[spots[0] * dests : (spots[-1] + 1) * dests]

    def place(step, me):
        return 0, part * blocks + (step if whole else (me[0] // dests) ^ (spots[0] + step))

    column = pl.BlockSpec((tokens, LANES), place)
    if whole:
        piece = pl.BlockSpec((dests, inner, 2, local, LANES), lambda step, me: (step, 0, 0, 0, 0))
    else:
        piece = pl.BlockSpec(pieces[0].shape, lambda step, me: (0, 0, 0, 0))
    return pl.pallas_call(
        functools.partial(finish_kernel, len(pieces)),
        out_shape=[jax.ShapeDtypeStruct(key_proj.shape, bf16)] * 4,
        grid_spec=pltpu.PrefetchScalarGridSpec(
            num_scalar_prefetch=1,
            grid=(len(spots),),
            in_specs=[pl.BlockSpec((1, LANES), place)]
            + [column] * 4
            + [piece] * len(pieces)
            + [pl.BlockSpec(memory_space=pl.ANY)] * len(previous),
            out_specs=[column] * 4,
            scratch_shapes=[pltpu.VMEM((2, LANES * (local + 1), LANES), f32)],
        ),
        input_output_aliases={6 + len(pieces) + index: index for index in range(len(previous))},
        compiler_params=pltpu.CompilerParams(vmem_limit_bytes=VMEM_BYTES),
        cost_estimate=pl.CostEstimate(flops=0, bytes_accessed=2**20, transcendentals=0),
        name="finish",
    )(me, skip, key_proj, value_proj, query_proj, out_grad, *pieces, *previous)


def swap(value, axis="ctx"):
    return lax.all_to_all(value, axis, split_axis=0, concat_axis=0, tiled=True)


def tie(values, *others):
    return lax.optimization_barrier((values, others))[0]


def exchange(pieces, axis, order=None):
    count = len(pieces)
    taken = list(pieces)
    for step in order or range(1, count):
        taken[step] = lax.ppermute(pieces[step], axis, [(i, i ^ step) for i in range(count)])
    return taken


def fast_shards(query_proj, key_proj, value_proj, out_grad, long_filter, skip_gain, parts):
    groups, planes = lax.axis_size("ctx"), lax.axis_size("ch")
    tokens, width = key_proj.shape
    channels, taps = long_filter.shape
    rows = groups * tokens // LANES
    local, tiles = tokens // LANES, taps // LANES
    inner = width // (groups * parts)
    tables = make_tables(rows)
    lead_taps = tables[0].reshape(2 * rows, 2, planes * groups, tiles).transpose(0, 1, 3, 2)
    lead_taps = jnp.asarray(lead_taps.reshape(2 * rows, 2 * rows))
    lead_fwd, lead_inv, trail_fwd, trail_inv, twist = (jnp.asarray(table) for table in tables)
    me = lax.axis_index("ctx")
    place = jnp.full((1,), me, jnp.int32)

    sources = jnp.arange(groups) ^ me
    lead = jnp.take(lead_fwd.reshape(2 * rows, 2, groups, local), sources, axis=2)
    lead = lead.reshape(lead_fwd.shape)
    back = jnp.take(lead_inv.reshape(2, groups, local, 2 * rows), sources, axis=1)
    back = back.reshape(lead_inv.shape)

    skip = skip_gain.reshape(1, width)
    shaped = long_filter.reshape(planes, parts, groups, inner, taps)
    gates = [
        gate(place, key_proj, value_proj, query_proj, out_grad, part, groups, inner)
        for part in range(parts)
    ]
    late = (1, groups - 1)

    slabs = [shaped[:, 0]] + [tie(shaped, gates[0])[:, part] for part in range(1, parts)]

    def send_filter(part, *others):
        slab = slabs[part].reshape(planes * groups, inner, taps)
        return swap(tie(slab, *others), ("ch", "ctx"))

    def spectrum_of(taps):
        return filter_spectrum([taps[:, None]], lead_taps, trail_fwd, twist, TILE)

    filters = send_filter(0)
    signals = exchange(gates[0], "ctx")
    outputs = []
    for part in range(parts):
        last = part == parts - 1
        if not last:
            following = send_filter(part + 1, filters, signals, gates[part + 1])
            early = [step for step in range(1, groups) if step not in late]
            pieces = tie(gates[part + 1], filters, signals)
            coming = exchange(pieces, "ctx", early)
        if not part:
            spectrum = spectrum_of(filters)
        tables = (lead, back if last else lead_inv, trail_fwd, trail_inv, twist)
        conv = convolve(signals, spectrum, tables, TILE, not last)
        if last:
            taken = exchange(conv, "ctx")
        else:
            for step in late:
                coming[step] = tie(pieces[step], conv[0])
            rest = exchange(coming, "ctx", late)
            coming = [rest[step] if step in late else coming[step] for step in range(groups)]
            conv, following = lax.optimization_barrier((conv[0], following))
            spectrum = spectrum_of(following)
            taken = [swap(tie(conv, spectrum, coming))]
            filters, signals = following, coming
        blocks = range(groups * inner // LANES)
        for spots in (blocks[:-1], blocks[-1:]) if last else (blocks,):
            outputs = finish(
                place, skip, taken, spots, key_proj, value_proj, query_proj, out_grad, part,
                groups, outputs,
            )
    return tuple(outputs)


def plain_shards(query_proj, key_proj, value_proj, out_grad, long_filter, skip_gain):
    groups, planes = lax.axis_size("ctx"), lax.axis_size("ch")
    tokens, width = key_proj.shape
    channels, taps = long_filter.shape
    inner = width // groups
    length = groups * tokens
    rows = length // LANES
    tables = tuple(jnp.asarray(table) for table in make_tables(rows))
    group = 2 if inner % 2 == 0 else 1
    sent = long_filter.reshape(planes, groups, inner, taps).transpose(1, 0, 2, 3)
    taken = swap(swap(sent).transpose(1, 0, 2, 3), "ch")
    filters = taken.transpose(2, 0, 1, 3).reshape(inner, rows, LANES)
    lead, twist = tables[0].astype(f32), tables[4]
    lead = lead[:, :rows] + lead[:, rows:]
    trail = tables[2].astype(f32)[2 * LANES :]
    trail = trail[: 2 * LANES] + trail[2 * LANES :]
    highest = lax.Precision.HIGHEST
    turned = jnp.einsum("kn,cnm->ckm", lead, filters.astype(f32), precision=highest)
    real, imag = turned[:, :rows], turned[:, rows:]
    turned = jnp.concatenate(
        [real * twist[0] - imag * twist[1], real * twist[1] + imag * twist[0]], 2
    )
    spectrum = jnp.einsum("ckm,mj->ckj", turned, trail, precision=highest)
    gated_kv = (key_proj.astype(f32) * value_proj.astype(f32)).astype(bf16)
    grad_gate = (out_grad.astype(f32) * query_proj.astype(f32)).astype(bf16)
    both = jnp.stack([gated_kv.T, grad_gate.T], 1)
    taken = swap(both.reshape(groups, inner, 2, tokens))
    signals = taken.transpose(1, 2, 0, 3).reshape(inner, 2, rows, LANES)
    (conv,) = convolve([signals], spectrum, tables, group)
    back = conv.reshape(inner, 2, groups, tokens).transpose(2, 0, 1, 3)
    back = swap(back).reshape(width, 2, tokens)
    convolved, reflected = back[:, 0].T, back[:, 1].T
    summed = convolved.astype(f32) + skip_gain[None, :] * gated_kv.astype(f32)
    grad_sum = reflected.astype(f32) + skip_gain[None, :] * grad_gate.astype(f32)
    return (
        (query_proj.astype(f32) * summed).astype(bf16),
        (out_grad.astype(f32) * summed).astype(bf16),
        (grad_sum * value_proj.astype(f32)).astype(bf16),
        (grad_sum * key_proj.astype(f32)).astype(bf16),
    )


def shards(query_proj, key_proj, value_proj, out_grad, long_filter, skip_gain):
    groups = lax.axis_size("ctx")
    tokens, width = key_proj.shape
    planes = lax.axis_size("ch")
    taps = long_filter.shape[1]
    args = (query_proj, key_proj, value_proj, out_grad, long_filter, skip_gain)
    parts = 2
    inner = width // (groups * parts)
    fits = (
        tokens % (TILE * LANES) == 0
        and taps % LANES == 0
        and width % (groups * parts) == 0
        and inner % TILE == 0
        and LANES % inner == 0
        and groups % (LANES // inner) == 0
        and planes & (planes - 1) == 0
        and groups & (groups - 1) == 0
    )
    if fits:
        return fast_shards(*args, parts)
    return plain_shards(*args)


def solution(mesh):
    placed = (
        P("ctx", "ch"),
        P("ctx", "ch"),
        P("ctx", "ch"),
        P("ctx", "ch"),
        P(None, ("ch", "ctx")),
        P("ch"),
    )
    return jax.shard_map(
        shards,
        mesh=mesh,
        in_specs=placed,
        out_specs=(P("ctx", "ch"), P("ctx", "ch"), P("ctx", "ch"), P("ctx", "ch")),
        check_vma=False,
    )
```

```python
import functools
import math

import jax
import jax.numpy as jnp
import ml_dtypes
import numpy as np
from jax import lax
from jax.experimental import pallas as pl
from jax.experimental.pallas import tpu as pltpu
from jax.sharding import PartitionSpec as P

LANES = 128
TILE = 16
VMEM_BYTES = 56 * 1024 * 1024

f32 = jnp.float32
bf16 = jnp.bfloat16


def two_parts(matrix):
    high = matrix.astype(ml_dtypes.bfloat16)
    low = (matrix - high.astype(np.float64)).astype(ml_dtypes.bfloat16)
    return high, low


def make_tables(rows):
    points = rows * LANES
    n1, k1 = np.arange(rows), np.arange(rows)
    n2, k2 = np.arange(LANES), np.arange(LANES)
    lead = 2 * math.pi / rows * np.outer(k1 + 0.25, n1)
    twist = 2 * math.pi / points * np.outer(k1 + 0.25, n2)
    trail = 2 * math.pi / LANES * np.outer(n2, k2)
    lead_fwd = np.concatenate([np.cos(lead), -np.sin(lead)], 0)
    lead_inv = np.concatenate([np.cos(lead).T, -np.sin(lead).T], 1) / points
    cosine, sine = np.cos(trail), np.sin(trail)
    trail_fwd = np.block([[cosine, -sine], [sine, cosine]])
    trail_inv = np.block([[cosine, sine], [-sine, cosine]])
    lead_fwd = np.concatenate(two_parts(lead_fwd), 1)
    lead_inv = np.concatenate(two_parts(lead_inv), 0)
    high, low = two_parts(trail_fwd)
    trail_fwd = np.concatenate([high, high, low], 0)
    high, low = two_parts(trail_inv)
    trail_inv = np.concatenate([high, high, low], 0)
    twist = np.stack([np.cos(twist), -np.sin(twist)]).astype(np.float32)
    return lead_fwd, lead_inv, trail_fwd, trail_inv, twist


def dot(left, right):
    return jnp.dot(left, right, preferred_element_type=f32)


def split(value):
    high = value.astype(bf16)
    return high, (value - high.astype(f32)).astype(bf16)


def lead_stage(lead, twist, pair):
    rows = pair.shape[0]
    turned = dot(lead, jnp.concatenate([pair, pair], 0))
    real, imag = turned[:rows], turned[rows:]
    parts = []
    for side in range(2):
        lanes = slice(side * LANES, (side + 1) * LANES)
        re, im = real[:, lanes], imag[:, lanes]
        parts.append(
            jnp.concatenate([re * twist[0] - im * twist[1], re * twist[1] + im * twist[0]], 1)
        )
    return parts


def store_split(ref, place, value):
    high, low = split(value)
    width = value.shape[1]
    ref[place, :width] = high
    ref[place, width : 2 * width] = low
    ref[place, 2 * width :] = high


def spectrum_kernel(pieces, group, lead_ref, trail_ref, twist_ref, *refs):
    taps = refs[:pieces]
    out_ref, scratch, wide = refs[pieces:]
    sources, _, _, width = taps[0].shape
    count = pieces * sources
    for piece in range(pieces):
        for source in range(sources):
            row = (piece * sources + source) * group
            for part in range(width // LANES):
                lanes = slice(part * LANES, (part + 1) * LANES)
                scratch[part, row : row + group, :] = taps[piece][source, 0, :, lanes].astype(f32)
    lead, twist = lead_ref[...], (twist_ref[0], twist_ref[1])
    rows = count * (width // LANES)

    def channel(index):
        parts = [
            scratch[part, pl.ds(index, count, stride=group), :] for part in range(width // LANES)
        ]
        return jnp.concatenate(parts, 0).astype(bf16)

    for index in range(0, group, 2):
        pair = jnp.concatenate([channel(index), channel(index + 1)], 1)
        for side, value in enumerate(lead_stage(lead, twist, pair)):
            place = slice((index + side) * rows, (index + side + 1) * rows)
            store_split(wide, place, value)
    step = 4
    for index in range(0, group, step):
        product = dot(wide[index * rows : (index + step) * rows, :], trail_ref[...])
        out_ref[index : index + step] = product.reshape(step, rows, 2 * LANES)


def filter_spectrum(pieces, lead, trail, twist, group):
    sources, outer, inner, width = pieces[0].shape
    rows = lead.shape[1] // 2
    steps = inner // group
    whole = lambda ndim: (lambda *_: (0,) * ndim)
    return pl.pallas_call(
        functools.partial(spectrum_kernel, len(pieces), group),
        out_shape=jax.ShapeDtypeStruct((outer * inner, rows, 2 * LANES), f32),
        grid=(outer * steps,),
        in_specs=[
            pl.BlockSpec(lead.shape, whole(2)),
            pl.BlockSpec(trail.shape, whole(2)),
            pl.BlockSpec(twist.shape, whole(3)),
        ]
        + [
            pl.BlockSpec(
                (sources, 1, group, width), lambda step: (0, step // steps, step % steps, 0)
            )
        ]
        * len(pieces),
        out_specs=pl.BlockSpec((group, rows, 2 * LANES), lambda step: (step, 0, 0)),
        scratch_shapes=[
            pltpu.VMEM((width // LANES, (len(pieces) * sources + 1) * group, LANES), f32),
            pltpu.VMEM((group * rows, 6 * LANES), bf16),
        ],
        compiler_params=pltpu.CompilerParams(vmem_limit_bytes=VMEM_BYTES),
        cost_estimate=pl.CostEstimate(
            flops=outer * inner * 10**6, bytes_accessed=2**20, transcendentals=0
        ),
        name="filter_spectrum",
    )(lead, trail, twist, *pieces)


def convolve_kernel(
    group, sources, lead_ref, inv_ref, trail_ref, back_ref, twist_ref, filter_ref, *refs
):
    signals, outs, (wide, spectra) = refs[:sources], refs[sources:-2], refs[-2:]
    local = signals[0].shape[2]
    rows = sources * local
    lead, inv, twist = lead_ref[...], inv_ref[...], (twist_ref[0], twist_ref[1])
    for index in range(group):
        pair = jnp.concatenate(
            [jnp.concatenate([ref[index, side] for ref in signals], 0) for side in range(2)], 1
        )
        for side, value in enumerate(lead_stage(lead, twist, pair)):
            place = slice((2 * index + side) * rows, (2 * index + side + 1) * rows)
            store_split(wide, place, value)
    for row in range(0, wide.shape[0], 512):
        spectra[row : row + 512, :] = dot(wide[row : row + 512, :], trail_ref[...])
    for index in range(group):
        fre, fim = filter_ref[index, :, :LANES], filter_ref[index, :, LANES:]
        for side in range(2):
            place = slice((2 * index + side) * rows, (2 * index + side + 1) * rows)
            re, im = spectra[place, :LANES], spectra[place, LANES:]
            if side == 0:
                product = jnp.concatenate([re * fre - im * fim, re * fim + im * fre], 1)
            else:
                product = jnp.concatenate([re * fre + im * fim, im * fre - re * fim], 1)
            store_split(wide, place, product)
    for row in range(0, wide.shape[0], 512):
        spectra[row : row + 512, :] = dot(wide[row : row + 512, :], back_ref[...])
    for index in range(group):
        reals, imags = [], []
        for side in range(2):
            place = slice((2 * index + side) * rows, (2 * index + side + 1) * rows)
            re, im = spectra[place, :LANES], spectra[place, LANES:]
            reals.append(re * twist[0] + im * twist[1])
            imags.append(im * twist[0] - re * twist[1])
        turned = jnp.concatenate([jnp.concatenate(reals, 1), jnp.concatenate(imags, 1)], 0)
        top, rest = split(turned)
        both = dot(inv, top)
        result = both[:rows] + both[rows:] + dot(inv[:rows], rest)
        result = result.astype(bf16)
        for side in range(2):
            lanes = slice(side * LANES, (side + 1) * LANES)
            for source in range(sources):
                value = result[source * local : (source + 1) * local, lanes]
                if len(outs[0].shape) == 5:
                    outs[0][source, index, side] = value
                else:
                    outs[source][index, side] = value


def convolve(signals, spectrum, tables, group, whole_out=False):
    lead_fwd, lead_inv, trail_fwd, trail_inv, twist = tables
    sources = len(signals)
    inner, _, local, _ = signals[0].shape
    rows = sources * local
    whole = lambda ndim: (lambda *_: (0,) * ndim)
    piece = pl.BlockSpec((group, 2, local, LANES), lambda step: (step, 0, 0, 0))
    if whole_out:
        out_shape = [jax.ShapeDtypeStruct((sources, inner, 2, local, LANES), bf16)]
        out_specs = [
            pl.BlockSpec((sources, group, 2, local, LANES), lambda step: (0, step, 0, 0, 0))
        ]
    else:
        out_shape = [jax.ShapeDtypeStruct((inner, 2, local, LANES), bf16)] * sources
        out_specs = [piece] * sources
    return pl.pallas_call(
        functools.partial(convolve_kernel, group, sources),
        out_shape=out_shape,
        grid=(inner // group,),
        in_specs=[
            pl.BlockSpec(lead_fwd.shape, whole(2)),
            pl.BlockSpec(lead_inv.shape, whole(2)),
            pl.BlockSpec(trail_fwd.shape, whole(2)),
            pl.BlockSpec(trail_inv.shape, whole(2)),
            pl.BlockSpec(twist.shape, whole(3)),
            pl.BlockSpec((group, rows, 2 * LANES), lambda step: (step, 0, 0)),
        ]
        + [piece] * sources,
        out_specs=out_specs,
        scratch_shapes=[
            pltpu.VMEM((2 * group * rows, 6 * LANES), bf16),
            pltpu.VMEM((2 * group * rows, 2 * LANES), f32),
        ],
        compiler_params=pltpu.CompilerParams(vmem_limit_bytes=VMEM_BYTES),
        cost_estimate=pl.CostEstimate(
            flops=inner * 10**6, bytes_accessed=2**20, transcendentals=0
        ),
        name="convolve",
    )(lead_fwd, lead_inv, trail_fwd, trail_inv, twist, spectrum, *signals)


def gate_kernel(me_ref, key_ref, value_ref, query_ref, grad_ref, *refs):
    outs, scratch = refs[:-1], refs[-1]
    tokens, width = key_ref.shape
    local = tokens // LANES
    pitch = LANES + 8
    inner = outs[0].shape[0]
    dests = width // inner
    mine = lax.rem(me_ref[0], dests)
    for side, (one, two) in enumerate(((key_ref, value_ref), (grad_ref, query_ref))):
        for row in range(local):
            place = slice(row * LANES, (row + 1) * LANES)
            product = one[place, :].astype(f32) * two[place, :].astype(f32)
            scratch[side, row * pitch : row * pitch + width, :] = product.T
    for block in range(len(outs) // dests):

        @pl.when(pl.program_id(0) == block)
        def _():
            for slot in range(dests):
                base = (mine ^ slot) * inner
                for side in range(2):
                    for index in range(inner):
                        outs[block * dests + slot][index, side] = scratch[
                            side, pl.ds(base + index, local, stride=pitch), :
                        ].astype(bf16)


def gate(me, key_proj, value_proj, query_proj, out_grad, part, groups, inner):
    tokens = key_proj.shape[0]
    local = tokens // LANES
    dests = LANES // inner
    blocks = groups // dests
    column = pl.BlockSpec(
        (tokens, LANES), lambda step, me: (0, part * blocks + ((me[0] // dests) ^ step))
    )
    piece = (inner, 2, local, LANES)
    return pl.pallas_call(
        gate_kernel,
        out_shape=[jax.ShapeDtypeStruct(piece, bf16)] * groups,
        grid_spec=pltpu.PrefetchScalarGridSpec(
            num_scalar_prefetch=1,
            grid=(blocks,),
            in_specs=[column] * 4,
            out_specs=[pl.BlockSpec(piece, lambda step, me: (0, 0, 0, 0))] * groups,
            scratch_shapes=[pltpu.VMEM((2, local * (LANES + 8) + LANES, LANES), f32)],
        ),
        compiler_params=pltpu.CompilerParams(vmem_limit_bytes=VMEM_BYTES),
        cost_estimate=pl.CostEstimate(flops=0, bytes_accessed=2**20, transcendentals=0),
        name="gate",
    )(me, key_proj, value_proj, query_proj, out_grad)


def finish_kernel(pieces_count, me_ref, skip_ref, key_ref, value_ref, query_ref, grad_ref, *refs):
    pieces = refs[:pieces_count]
    out_ref, query_out, key_out, value_out, scratch = refs[-5:]
    tokens, width = key_ref.shape
    local = tokens // LANES
    pitch = local + 1
    inner = pieces[0].shape[-4]
    dests = width // inner
    mine = lax.rem(me_ref[0], dests)
    skip = skip_ref[...]
    if pieces_count == 1:
        for slot in range(dests):
            for side in range(2):
                for index in range(inner):
                    row = (slot * inner + index) * pitch
                    scratch[side, row : row + local, :] = pieces[0][slot, index, side].astype(f32)
    for block in range(pieces_count // dests):

        @pl.when(pl.program_id(0) == block)
        def _():
            for slot in range(dests):
                base = (mine ^ slot) * (inner * pitch)
                for side in range(2):
                    for index in range(inner):
                        scratch[side, pl.ds(base + index * pitch, local), :] = pieces[
                            block * dests + slot
                        ][index, side].astype(f32)

    for row in range(local):
        place = slice(row * LANES, (row + 1) * LANES)
        key, value = key_ref[place, :].astype(f32), value_ref[place, :].astype(f32)
        query, grad = query_ref[place, :].astype(f32), grad_ref[place, :].astype(f32)
        convolved = scratch[0, pl.ds(row, width, stride=pitch), :].T
        reflected = scratch[1, pl.ds(row, width, stride=pitch), :].T
        summed = convolved + skip * (key * value).astype(bf16).astype(f32)
        grad_sum = reflected + skip * (grad * query).astype(bf16).astype(f32)
        out_ref[place, :] = (query * summed).astype(bf16)
        query_out[place, :] = (grad * summed).astype(bf16)
        key_out[place, :] = (grad_sum * value).astype(bf16)
        value_out[place, :] = (grad_sum * key).astype(bf16)


def finish(me, skip, pieces, spots, key_proj, value_proj, query_proj, out_grad, part, groups, previous):
    inner, _, local, _ = pieces[0].shape[-4:]
    tokens = key_proj.shape[0]
    dests = LANES // inner
    blocks = groups // dests
    whole = len(pieces) == 1
    if not whole:
        pieces = pieces[spots[0] * dests : (spots[-1] + 1) * dests]

    def place(step, me):
        return 0, part * blocks + (step if whole else (me[0] // dests) ^ (spots[0] + step))

    column = pl.BlockSpec((tokens, LANES), place)
    if whole:
        piece = pl.BlockSpec((dests, inner, 2, local, LANES), lambda step, me: (step, 0, 0, 0, 0))
    else:
        piece = pl.BlockSpec(pieces[0].shape, lambda step, me: (0, 0, 0, 0))
    return pl.pallas_call(
        functools.partial(finish_kernel, len(pieces)),
        out_shape=[jax.ShapeDtypeStruct(key_proj.shape, bf16)] * 4,
        grid_spec=pltpu.PrefetchScalarGridSpec(
            num_scalar_prefetch=1,
            grid=(len(spots),),
            in_specs=[pl.BlockSpec((1, LANES), place)]
            + [column] * 4
            + [piece] * len(pieces)
            + [pl.BlockSpec(memory_space=pl.ANY)] * len(previous),
            out_specs=[column] * 4,
            scratch_shapes=[pltpu.VMEM((2, LANES * (local + 1) + local + 8, LANES), f32)],
        ),
        input_output_aliases={6 + len(pieces) + index: index for index in range(len(previous))},
        compiler_params=pltpu.CompilerParams(vmem_limit_bytes=VMEM_BYTES),
        cost_estimate=pl.CostEstimate(flops=0, bytes_accessed=2**20, transcendentals=0),
        name="finish",
    )(me, skip, key_proj, value_proj, query_proj, out_grad, *pieces, *previous)


def swap(value, axis="ctx"):
    return lax.all_to_all(value, axis, split_axis=0, concat_axis=0, tiled=True)


def tie(values, *others):
    return lax.optimization_barrier((values, others))[0]


def exchange(pieces, axis, order=None):
    count = len(pieces)
    taken = list(pieces)
    for step in order or range(1, count):
        taken[step] = lax.ppermute(pieces[step], axis, [(i, i ^ step) for i in range(count)])
    return taken


def fast_shards(query_proj, key_proj, value_proj, out_grad, long_filter, skip_gain, parts):
    groups, planes = lax.axis_size("ctx"), lax.axis_size("ch")
    tokens, width = key_proj.shape
    channels, taps = long_filter.shape
    rows = groups * tokens // LANES
    local, tiles = tokens // LANES, taps // LANES
    inner = width // (groups * parts)
    tables = make_tables(rows)
    lead_taps = tables[0].reshape(2 * rows, 2, planes * groups, tiles).transpose(0, 1, 3, 2)
    lead_taps = jnp.asarray(lead_taps.reshape(2 * rows, 2 * rows))
    lead_fwd, lead_inv, trail_fwd, trail_inv, twist = (jnp.asarray(table) for table in tables)
    me = lax.axis_index("ctx")
    place = jnp.full((1,), me, jnp.int32)

    sources = jnp.arange(groups) ^ me
    lead = jnp.take(lead_fwd.reshape(2 * rows, 2, groups, local), sources, axis=2)
    lead = lead.reshape(lead_fwd.shape)
    back = jnp.take(lead_inv.reshape(2, groups, local, 2 * rows), sources, axis=1)
    back = back.reshape(lead_inv.shape)

    skip = skip_gain.reshape(1, width)
    shaped = long_filter.reshape(planes, parts, groups, inner, taps)
    gates = [
        gate(place, key_proj, value_proj, query_proj, out_grad, part, groups, inner)
        for part in range(parts)
    ]
    late = (1, groups - 1)

    slabs = [shaped[:, 0]] + [tie(shaped, gates[0])[:, part] for part in range(1, parts)]

    def send_filter(part, *others):
        slab = slabs[part].reshape(planes * groups, inner, taps)
        return swap(tie(slab, *others), ("ch", "ctx"))

    def spectrum_of(taps):
        return filter_spectrum([taps[:, None]], lead_taps, trail_fwd, twist, TILE)

    filters = send_filter(0)
    signals = exchange(gates[0], "ctx")
    outputs = []
    for part in range(parts):
        last = part == parts - 1
        if not last:
            following = send_filter(part + 1, filters, signals, gates[part + 1])
            early = [step for step in range(1, groups) if step not in late]
            pieces = tie(gates[part + 1], filters, signals)
            coming = exchange(pieces, "ctx", early)
        if not part:
            spectrum = spectrum_of(filters)
        tables = (lead, back if last else lead_inv, trail_fwd, trail_inv, twist)
        conv = convolve(signals, spectrum, tables, TILE, not last)
        if last:
            taken = exchange(conv, "ctx")
        else:
            for step in late:
                coming[step] = tie(pieces[step], conv[0])
            rest = exchange(coming, "ctx", late)
            coming = [rest[step] if step in late else coming[step] for step in range(groups)]
            conv, following = lax.optimization_barrier((conv[0], following))
            spectrum = spectrum_of(following)
            taken = [swap(tie(conv, spectrum, coming))]
            filters, signals = following, coming
        blocks = range(groups * inner // LANES)
        for spots in (blocks[:-1], blocks[-1:]) if last else (blocks,):
            outputs = finish(
                place, skip, taken, spots, key_proj, value_proj, query_proj, out_grad, part,
                groups, outputs,
            )
    return tuple(outputs)


def plain_shards(query_proj, key_proj, value_proj, out_grad, long_filter, skip_gain):
    groups, planes = lax.axis_size("ctx"), lax.axis_size("ch")
    tokens, width = key_proj.shape
    channels, taps = long_filter.shape
    inner = width // groups
    length = groups * tokens
    rows = length // LANES
    tables = tuple(jnp.asarray(table) for table in make_tables(rows))
    group = 2 if inner % 2 == 0 else 1
    sent = long_filter.reshape(planes, groups, inner, taps).transpose(1, 0, 2, 3)
    taken = swap(swap(sent).transpose(1, 0, 2, 3), "ch")
    filters = taken.transpose(2, 0, 1, 3).reshape(inner, rows, LANES)
    lead, twist = tables[0].astype(f32), tables[4]
    lead = lead[:, :rows] + lead[:, rows:]
    trail = tables[2].astype(f32)[2 * LANES :]
    trail = trail[: 2 * LANES] + trail[2 * LANES :]
    highest = lax.Precision.HIGHEST
    turned = jnp.einsum("kn,cnm->ckm", lead, filters.astype(f32), precision=highest)
    real, imag = turned[:, :rows], turned[:, rows:]
    turned = jnp.concatenate(
        [real * twist[0] - imag * twist[1], real * twist[1] + imag * twist[0]], 2
    )
    spectrum = jnp.einsum("ckm,mj->ckj", turned, trail, precision=highest)
    gated_kv = (key_proj.astype(f32) * value_proj.astype(f32)).astype(bf16)
    grad_gate = (out_grad.astype(f32) * query_proj.astype(f32)).astype(bf16)
    both = jnp.stack([gated_kv.T, grad_gate.T], 1)
    taken = swap(both.reshape(groups, inner, 2, tokens))
    signals = taken.transpose(1, 2, 0, 3).reshape(inner, 2, rows, LANES)
    (conv,) = convolve([signals], spectrum, tables, group)
    back = conv.reshape(inner, 2, groups, tokens).transpose(2, 0, 1, 3)
    back = swap(back).reshape(width, 2, tokens)
    convolved, reflected = back[:, 0].T, back[:, 1].T
    summed = convolved.astype(f32) + skip_gain[None, :] * gated_kv.astype(f32)
    grad_sum = reflected.astype(f32) + skip_gain[None, :] * grad_gate.astype(f32)
    return (
        (query_proj.astype(f32) * summed).astype(bf16),
        (out_grad.astype(f32) * summed).astype(bf16),
        (grad_sum * value_proj.astype(f32)).astype(bf16),
        (grad_sum * key_proj.astype(f32)).astype(bf16),
    )


def shards(query_proj, key_proj, value_proj, out_grad, long_filter, skip_gain):
    groups = lax.axis_size("ctx")
    tokens, width = key_proj.shape
    planes = lax.axis_size("ch")
    taps = long_filter.shape[1]
    args = (query_proj, key_proj, value_proj, out_grad, long_filter, skip_gain)
    parts = 2
    inner = width // (groups * parts)
    fits = (
        tokens % (TILE * LANES) == 0
        and taps % LANES == 0
        and width % (groups * parts) == 0
        and inner % TILE == 0
        and LANES % inner == 0
        and groups % (LANES // inner) == 0
        and planes & (planes - 1) == 0
        and groups & (groups - 1) == 0
    )
    if fits:
        return fast_shards(*args, parts)
    return plain_shards(*args)


def solution(mesh):
    placed = (
        P("ctx", "ch"),
        P("ctx", "ch"),
        P("ctx", "ch"),
        P("ctx", "ch"),
        P(None, ("ch", "ctx")),
        P("ch"),
    )
    return jax.shard_map(
        shards,
        mesh=mesh,
        in_specs=placed,
        out_specs=(P("ctx", "ch"), P("ctx", "ch"), P("ctx", "ch"), P("ctx", "ch")),
        check_vma=False,
    )
```

```python
import functools
import math

import jax
import jax.numpy as jnp
import ml_dtypes
import numpy as np
from jax import lax
from jax.experimental import pallas as pl
from jax.experimental.pallas import tpu as pltpu
from jax.sharding import PartitionSpec as P

LANES = 128
TILE = 16
VMEM_BYTES = 56 * 1024 * 1024

f32 = jnp.float32
bf16 = jnp.bfloat16


def two_parts(matrix):
    high = matrix.astype(ml_dtypes.bfloat16)
    low = (matrix - high.astype(np.float64)).astype(ml_dtypes.bfloat16)
    return high, low


def make_tables(rows):
    points = rows * LANES
    n1, k1 = np.arange(rows), np.arange(rows)
    n2, k2 = np.arange(LANES), np.arange(LANES)
    lead = 2 * math.pi / rows * np.outer(k1 + 0.25, n1)
    twist = 2 * math.pi / points * np.outer(k1 + 0.25, n2)
    trail = 2 * math.pi / LANES * np.outer(n2, k2)
    lead_fwd = np.concatenate([np.cos(lead), -np.sin(lead)], 0)
    lead_inv = np.concatenate([np.cos(lead).T, -np.sin(lead).T], 1) / points
    cosine, sine = np.cos(trail), np.sin(trail)
    trail_fwd = np.block([[cosine, -sine], [sine, cosine]])
    trail_inv = np.block([[cosine, sine], [-sine, cosine]])
    lead_fwd = np.concatenate(two_parts(lead_fwd), 1)
    lead_inv = np.concatenate(two_parts(lead_inv), 0)
    high, low = two_parts(trail_fwd)
    trail_fwd = np.concatenate([high, high, low], 0)
    high, low = two_parts(trail_inv)
    trail_inv = np.concatenate([high, high, low], 0)
    twist = np.stack([np.cos(twist), -np.sin(twist)]).astype(np.float32)
    return lead_fwd, lead_inv, trail_fwd, trail_inv, twist


def dot(left, right):
    return jnp.dot(left, right, preferred_element_type=f32)


def split(value):
    high = value.astype(bf16)
    return high, (value - high.astype(f32)).astype(bf16)


def lead_stage(lead, twist, pair):
    rows = pair.shape[0]
    turned = dot(lead, jnp.concatenate([pair, pair], 0))
    real, imag = turned[:rows], turned[rows:]
    parts = []
    for side in range(2):
        lanes = slice(side * LANES, (side + 1) * LANES)
        re, im = real[:, lanes], imag[:, lanes]
        parts.append(
            jnp.concatenate([re * twist[0] - im * twist[1], re * twist[1] + im * twist[0]], 1)
        )
    return parts


def store_split(ref, place, value):
    high, low = split(value)
    width = value.shape[1]
    ref[place, :width] = high
    ref[place, width : 2 * width] = low
    ref[place, 2 * width :] = high


def spectrum_kernel(pieces, group, lead_ref, trail_ref, twist_ref, *refs):
    taps = refs[:pieces]
    out_ref, scratch, wide = refs[pieces:]
    sources, _, _, width = taps[0].shape
    count = pieces * sources
    for piece in range(pieces):
        for source in range(sources):
            row = (piece * sources + source) * group
            for part in range(width // LANES):
                lanes = slice(part * LANES, (part + 1) * LANES)
                scratch[part, row : row + group, :] = taps[piece][source, 0, :, lanes].astype(f32)
    lead, twist = lead_ref[...], (twist_ref[0], twist_ref[1])
    rows = count * (width // LANES)

    def channel(index):
        parts = [
            scratch[part, pl.ds(index, count, stride=group), :] for part in range(width // LANES)
        ]
        return jnp.concatenate(parts, 0).astype(bf16)

    for index in range(0, group, 2):
        pair = jnp.concatenate([channel(index), channel(index + 1)], 1)
        for side, value in enumerate(lead_stage(lead, twist, pair)):
            place = slice((index + side) * rows, (index + side + 1) * rows)
            store_split(wide, place, value)
    step = 4
    for index in range(0, group, step):
        product = dot(wide[index * rows : (index + step) * rows, :], trail_ref[...])
        out_ref[index : index + step] = product.reshape(step, rows, 2 * LANES)


def filter_spectrum(pieces, lead, trail, twist, group):
    sources, outer, inner, width = pieces[0].shape
    rows = lead.shape[1] // 2
    steps = inner // group
    whole = lambda ndim: (lambda *_: (0,) * ndim)
    return pl.pallas_call(
        functools.partial(spectrum_kernel, len(pieces), group),
        out_shape=jax.ShapeDtypeStruct((outer * inner, rows, 2 * LANES), f32),
        grid=(outer * steps,),
        in_specs=[
            pl.BlockSpec(lead.shape, whole(2)),
            pl.BlockSpec(trail.shape, whole(2)),
            pl.BlockSpec(twist.shape, whole(3)),
        ]
        + [
            pl.BlockSpec(
                (sources, 1, group, width), lambda step: (0, step // steps, step % steps, 0)
            )
        ]
        * len(pieces),
        out_specs=pl.BlockSpec((group, rows, 2 * LANES), lambda step: (step, 0, 0)),
        scratch_shapes=[
            pltpu.VMEM((width // LANES, (len(pieces) * sources + 1) * group, LANES), f32),
            pltpu.VMEM((group * rows, 6 * LANES), bf16),
        ],
        compiler_params=pltpu.CompilerParams(vmem_limit_bytes=VMEM_BYTES),
        cost_estimate=pl.CostEstimate(
            flops=outer * inner * 10**6, bytes_accessed=2**20, transcendentals=0
        ),
        name="filter_spectrum",
    )(lead, trail, twist, *pieces)


def convolve_kernel(
    group, sources, lead_ref, inv_ref, trail_ref, back_ref, twist_ref, filter_ref, *refs
):
    signals, outs, (wide, spectra) = refs[:sources], refs[sources:-2], refs[-2:]
    local = signals[0].shape[2]
    rows = sources * local
    lead, inv, twist = lead_ref[...], inv_ref[...], (twist_ref[0], twist_ref[1])
    for index in range(group):
        pair = jnp.concatenate(
            [jnp.concatenate([ref[index, side] for ref in signals], 0) for side in range(2)], 1
        )
        for side, value in enumerate(lead_stage(lead, twist, pair)):
            place = slice((2 * index + side) * rows, (2 * index + side + 1) * rows)
            store_split(wide, place, value)
    for row in range(0, wide.shape[0], 512):
        spectra[row : row + 512, :] = dot(wide[row : row + 512, :], trail_ref[...])
    for index in range(group):
        fre, fim = filter_ref[index, :, :LANES], filter_ref[index, :, LANES:]
        for side in range(2):
            place = slice((2 * index + side) * rows, (2 * index + side + 1) * rows)
            re, im = spectra[place, :LANES], spectra[place, LANES:]
            if side == 0:
                product = jnp.concatenate([re * fre - im * fim, re * fim + im * fre], 1)
            else:
                product = jnp.concatenate([re * fre + im * fim, im * fre - re * fim], 1)
            store_split(wide, place, product)
    for row in range(0, wide.shape[0], 512):
        spectra[row : row + 512, :] = dot(wide[row : row + 512, :], back_ref[...])
    for index in range(group):
        reals, imags = [], []
        for side in range(2):
            place = slice((2 * index + side) * rows, (2 * index + side + 1) * rows)
            re, im = spectra[place, :LANES], spectra[place, LANES:]
            reals.append(re * twist[0] + im * twist[1])
            imags.append(im * twist[0] - re * twist[1])
        turned = jnp.concatenate([jnp.concatenate(reals, 1), jnp.concatenate(imags, 1)], 0)
        top, rest = split(turned)
        both = dot(inv, top)
        result = both[:rows] + both[rows:] + dot(inv[:rows], rest)
        result = result.astype(bf16)
        for side in range(2):
            lanes = slice(side * LANES, (side + 1) * LANES)
            for source in range(sources):
                value = result[source * local : (source + 1) * local, lanes]
                if len(outs[0].shape) == 5:
                    outs[0][source, index, side] = value
                else:
                    outs[source][index, side] = value


def convolve(signals, spectrum, tables, group, whole_out=False):
    lead_fwd, lead_inv, trail_fwd, trail_inv, twist = tables
    sources = len(signals)
    inner, _, local, _ = signals[0].shape
    rows = sources * local
    whole = lambda ndim: (lambda *_: (0,) * ndim)
    piece = pl.BlockSpec((group, 2, local, LANES), lambda step: (step, 0, 0, 0))
    if whole_out:
        out_shape = [jax.ShapeDtypeStruct((sources, inner, 2, local, LANES), bf16)]
        out_specs = [
            pl.BlockSpec((sources, group, 2, local, LANES), lambda step: (0, step, 0, 0, 0))
        ]
    else:
        out_shape = [jax.ShapeDtypeStruct((inner, 2, local, LANES), bf16)] * sources
        out_specs = [piece] * sources
    return pl.pallas_call(
        functools.partial(convolve_kernel, group, sources),
        out_shape=out_shape,
        grid=(inner // group,),
        in_specs=[
            pl.BlockSpec(lead_fwd.shape, whole(2)),
            pl.BlockSpec(lead_inv.shape, whole(2)),
            pl.BlockSpec(trail_fwd.shape, whole(2)),
            pl.BlockSpec(trail_inv.shape, whole(2)),
            pl.BlockSpec(twist.shape, whole(3)),
            pl.BlockSpec((group, rows, 2 * LANES), lambda step: (step, 0, 0)),
        ]
        + [piece] * sources,
        out_specs=out_specs,
        scratch_shapes=[
            pltpu.VMEM((2 * group * rows, 6 * LANES), bf16),
            pltpu.VMEM((2 * group * rows, 2 * LANES), f32),
        ],
        compiler_params=pltpu.CompilerParams(vmem_limit_bytes=VMEM_BYTES),
        cost_estimate=pl.CostEstimate(
            flops=inner * 10**6, bytes_accessed=2**20, transcendentals=0
        ),
        name="convolve",
    )(lead_fwd, lead_inv, trail_fwd, trail_inv, twist, spectrum, *signals)


def gate_kernel(me_ref, key_ref, value_ref, query_ref, grad_ref, *refs):
    outs, scratch = refs[:-1], refs[-1]
    tokens, width = key_ref.shape
    local = tokens // LANES
    pitch = LANES + 8
    inner = outs[0].shape[0]
    dests = width // inner
    mine = lax.rem(me_ref[0], dests)
    for side, (one, two) in enumerate(((key_ref, value_ref), (grad_ref, query_ref))):
        for row in range(local):
            place = slice(row * LANES, (row + 1) * LANES)
            product = one[place, :].astype(f32) * two[place, :].astype(f32)
            scratch[side, row * pitch : row * pitch + width, :] = product.T
    for block in range(len(outs) // dests):

        @pl.when(pl.program_id(0) == block)
        def _():
            for slot in range(dests):
                base = (mine ^ slot) * inner
                for side in range(2):
                    for index in range(inner):
                        outs[block * dests + slot][index, side] = scratch[
                            side, pl.ds(base + index, local, stride=pitch), :
                        ].astype(bf16)


def gate(me, key_proj, value_proj, query_proj, out_grad, part, groups, inner):
    tokens = key_proj.shape[0]
    local = tokens // LANES
    dests = LANES // inner
    blocks = groups // dests
    column = pl.BlockSpec(
        (tokens, LANES), lambda step, me: (0, part * blocks + ((me[0] // dests) ^ step))
    )
    piece = (inner, 2, local, LANES)
    return pl.pallas_call(
        gate_kernel,
        out_shape=[jax.ShapeDtypeStruct(piece, bf16)] * groups,
        grid_spec=pltpu.PrefetchScalarGridSpec(
            num_scalar_prefetch=1,
            grid=(blocks,),
            in_specs=[column] * 4,
            out_specs=[pl.BlockSpec(piece, lambda step, me: (0, 0, 0, 0))] * groups,
            scratch_shapes=[pltpu.VMEM((2, local * (LANES + 8) + LANES, LANES), f32)],
        ),
        compiler_params=pltpu.CompilerParams(vmem_limit_bytes=VMEM_BYTES),
        cost_estimate=pl.CostEstimate(flops=0, bytes_accessed=2**20, transcendentals=0),
        name="gate",
    )(me, key_proj, value_proj, query_proj, out_grad)


def finish_kernel(pieces_count, me_ref, skip_ref, key_ref, value_ref, query_ref, grad_ref, *refs):
    pieces = refs[:pieces_count]
    out_ref, query_out, key_out, value_out, scratch = refs[-5:]
    share, width = key_ref.shape
    local = pieces[0].shape[-2]
    pitch = local + 1
    half = pl.program_id(1)
    inner = pieces[0].shape[-4]
    dests = width // inner
    mine = lax.rem(me_ref[0], dests)
    skip = skip_ref[...]
    if pieces_count == 1:

        @pl.when(half == 0)
        def _():
            for slot in range(dests):
                for side in range(2):
                    for index in range(inner):
                        row = (slot * inner + index) * pitch
                        scratch[side, row : row + local, :] = pieces[0][slot, index, side].astype(f32)

    for block in range(pieces_count // dests):

        @pl.when(jnp.logical_and(pl.program_id(0) == block, half == 0))
        def _():
            for slot in range(dests):
                base = (mine ^ slot) * (inner * pitch)
                for side in range(2):
                    for index in range(inner):
                        scratch[side, pl.ds(base + index * pitch, local), :] = pieces[
                            block * dests + slot
                        ][index, side].astype(f32)

    first = half * (share // LANES)
    for row in range(share // LANES):
        place = slice(row * LANES, (row + 1) * LANES)
        key, value = key_ref[place, :].astype(f32), value_ref[place, :].astype(f32)
        query, grad = query_ref[place, :].astype(f32), grad_ref[place, :].astype(f32)
        convolved = scratch[0, pl.ds(first + row, width, stride=pitch), :].T
        reflected = scratch[1, pl.ds(first + row, width, stride=pitch), :].T
        summed = convolved + skip * (key * value).astype(bf16).astype(f32)
        grad_sum = reflected + skip * (grad * query).astype(bf16).astype(f32)
        out_ref[place, :] = (query * summed).astype(bf16)
        query_out[place, :] = (grad * summed).astype(bf16)
        key_out[place, :] = (grad_sum * value).astype(bf16)
        value_out[place, :] = (grad_sum * key).astype(bf16)


def finish(me, skip, pieces, spots, key_proj, value_proj, query_proj, out_grad, part, groups, previous):
    inner, _, local, _ = pieces[0].shape[-4:]
    tokens = key_proj.shape[0]
    dests = LANES // inner
    blocks = groups // dests
    whole = len(pieces) == 1
    if not whole:
        pieces = pieces[spots[0] * dests : (spots[-1] + 1) * dests]

    def place(step, half, me):
        return half, part * blocks + (step if whole else (me[0] // dests) ^ (spots[0] + step))

    column = pl.BlockSpec((tokens // 2, LANES), place)
    if whole:
        piece = pl.BlockSpec((dests, inner, 2, local, LANES), lambda step, half, me: (step, 0, 0, 0, 0))
    else:
        piece = pl.BlockSpec(pieces[0].shape, lambda step, half, me: (0, 0, 0, 0))
    return pl.pallas_call(
        functools.partial(finish_kernel, len(pieces)),
        out_shape=[jax.ShapeDtypeStruct(key_proj.shape, bf16)] * 4,
        grid_spec=pltpu.PrefetchScalarGridSpec(
            num_scalar_prefetch=1,
            grid=(len(spots), 2),
            in_specs=[pl.BlockSpec((1, LANES), lambda step, half, me: (0, place(step, half, me)[1]))]
            + [column] * 4
            + [piece] * len(pieces)
            + [pl.BlockSpec(memory_space=pl.ANY)] * len(previous),
            out_specs=[column] * 4,
            scratch_shapes=[pltpu.VMEM((2, LANES * (local + 1) + local + 8, LANES), f32)],
        ),
        input_output_aliases={6 + len(pieces) + index: index for index in range(len(previous))},
        compiler_params=pltpu.CompilerParams(vmem_limit_bytes=VMEM_BYTES),
        cost_estimate=pl.CostEstimate(flops=0, bytes_accessed=2**20, transcendentals=0),
        name="finish",
    )(me, skip, key_proj, value_proj, query_proj, out_grad, *pieces, *previous)


def swap(value, axis="ctx"):
    return lax.all_to_all(value, axis, split_axis=0, concat_axis=0, tiled=True)


def tie(values, *others):
    return lax.optimization_barrier((values, others))[0]


def exchange(pieces, axis, order=None):
    count = len(pieces)
    taken = list(pieces)
    for step in order or range(1, count):
        taken[step] = lax.ppermute(pieces[step], axis, [(i, i ^ step) for i in range(count)])
    return taken


def fast_shards(query_proj, key_proj, value_proj, out_grad, long_filter, skip_gain, parts):
    groups, planes = lax.axis_size("ctx"), lax.axis_size("ch")
    tokens, width = key_proj.shape
    channels, taps = long_filter.shape
    rows = groups * tokens // LANES
    local, tiles = tokens // LANES, taps // LANES
    inner = width // (groups * parts)
    tables = make_tables(rows)
    lead_taps = tables[0].reshape(2 * rows, 2, planes * groups, tiles).transpose(0, 1, 3, 2)
    lead_taps = jnp.asarray(lead_taps.reshape(2 * rows, 2 * rows))
    lead_fwd, lead_inv, trail_fwd, trail_inv, twist = (jnp.asarray(table) for table in tables)
    me = lax.axis_index("ctx")
    place = jnp.full((1,), me, jnp.int32)

    sources = jnp.arange(groups) ^ me
    lead = jnp.take(lead_fwd.reshape(2 * rows, 2, groups, local), sources, axis=2)
    lead = lead.reshape(lead_fwd.shape)
    back = jnp.take(lead_inv.reshape(2, groups, local, 2 * rows), sources, axis=1)
    back = back.reshape(lead_inv.shape)

    skip = skip_gain.reshape(1, width)
    shaped = long_filter.reshape(planes, parts, groups, inner, taps)
    gates = [
        gate(place, key_proj, value_proj, query_proj, out_grad, part, groups, inner)
        for part in range(parts)
    ]
    late = (1, groups - 1)

    slabs = [shaped[:, 0]] + [tie(shaped, gates[0])[:, part] for part in range(1, parts)]

    def send_filter(part, *others):
        slab = slabs[part].reshape(planes * groups, inner, taps)
        return swap(tie(slab, *others), ("ch", "ctx"))

    def spectrum_of(taps):
        return filter_spectrum([taps[:, None]], lead_taps, trail_fwd, twist, TILE)

    filters = send_filter(0)
    signals = exchange(gates[0], "ctx")
    outputs = []
    for part in range(parts):
        last = part == parts - 1
        if not last:
            following = send_filter(part + 1, filters, signals, gates[part + 1])
            early = [step for step in range(1, groups) if step not in late]
            pieces = tie(gates[part + 1], filters, signals)
            coming = exchange(pieces, "ctx", early)
        if not part:
            spectrum = spectrum_of(filters)
        tables = (lead, back if last else lead_inv, trail_fwd, trail_inv, twist)
        conv = convolve(signals, spectrum, tables, TILE, not last)
        if last:
            taken = exchange(conv, "ctx")
        else:
            for step in late:
                coming[step] = tie(pieces[step], conv[0])
            rest = exchange(coming, "ctx", late)
            coming = [rest[step] if step in late else coming[step] for step in range(groups)]
            conv, following = lax.optimization_barrier((conv[0], following))
            spectrum = spectrum_of(following)
            taken = [swap(tie(conv, spectrum, coming))]
            filters, signals = following, coming
        blocks = range(groups * inner // LANES)
        for spots in (blocks[:-1], blocks[-1:]) if last else (blocks,):
            outputs = finish(
                place, skip, taken, spots, key_proj, value_proj, query_proj, out_grad, part,
                groups, outputs,
            )
    return tuple(outputs)


def plain_shards(query_proj, key_proj, value_proj, out_grad, long_filter, skip_gain):
    groups, planes = lax.axis_size("ctx"), lax.axis_size("ch")
    tokens, width = key_proj.shape
    channels, taps = long_filter.shape
    inner = width // groups
    length = groups * tokens
    rows = length // LANES
    tables = tuple(jnp.asarray(table) for table in make_tables(rows))
    group = 2 if inner % 2 == 0 else 1
    sent = long_filter.reshape(planes, groups, inner, taps).transpose(1, 0, 2, 3)
    taken = swap(swap(sent).transpose(1, 0, 2, 3), "ch")
    filters = taken.transpose(2, 0, 1, 3).reshape(inner, rows, LANES)
    lead, twist = tables[0].astype(f32), tables[4]
    lead = lead[:, :rows] + lead[:, rows:]
    trail = tables[2].astype(f32)[2 * LANES :]
    trail = trail[: 2 * LANES] + trail[2 * LANES :]
    highest = lax.Precision.HIGHEST
    turned = jnp.einsum("kn,cnm->ckm", lead, filters.astype(f32), precision=highest)
    real, imag = turned[:, :rows], turned[:, rows:]
    turned = jnp.concatenate(
        [real * twist[0] - imag * twist[1], real * twist[1] + imag * twist[0]], 2
    )
    spectrum = jnp.einsum("ckm,mj->ckj", turned, trail, precision=highest)
    gated_kv = (key_proj.astype(f32) * value_proj.astype(f32)).astype(bf16)
    grad_gate = (out_grad.astype(f32) * query_proj.astype(f32)).astype(bf16)
    both = jnp.stack([gated_kv.T, grad_gate.T], 1)
    taken = swap(both.reshape(groups, inner, 2, tokens))
    signals = taken.transpose(1, 2, 0, 3).reshape(inner, 2, rows, LANES)
    (conv,) = convolve([signals], spectrum, tables, group)
    back = conv.reshape(inner, 2, groups, tokens).transpose(2, 0, 1, 3)
    back = swap(back).reshape(width, 2, tokens)
    convolved, reflected = back[:, 0].T, back[:, 1].T
    summed = convolved.astype(f32) + skip_gain[None, :] * gated_kv.astype(f32)
    grad_sum = reflected.astype(f32) + skip_gain[None, :] * grad_gate.astype(f32)
    return (
        (query_proj.astype(f32) * summed).astype(bf16),
        (out_grad.astype(f32) * summed).astype(bf16),
        (grad_sum * value_proj.astype(f32)).astype(bf16),
        (grad_sum * key_proj.astype(f32)).astype(bf16),
    )


def shards(query_proj, key_proj, value_proj, out_grad, long_filter, skip_gain):
    groups = lax.axis_size("ctx")
    tokens, width = key_proj.shape
    planes = lax.axis_size("ch")
    taps = long_filter.shape[1]
    args = (query_proj, key_proj, value_proj, out_grad, long_filter, skip_gain)
    parts = 2
    inner = width // (groups * parts)
    fits = (
        tokens % (TILE * LANES) == 0
        and taps % LANES == 0
        and width % (groups * parts) == 0
        and inner % TILE == 0
        and LANES % inner == 0
        and groups % (LANES // inner) == 0
        and planes & (planes - 1) == 0
        and groups & (groups - 1) == 0
    )
    if fits:
        return fast_shards(*args, parts)
    return plain_shards(*args)


def solution(mesh):
    placed = (
        P("ctx", "ch"),
        P("ctx", "ch"),
        P("ctx", "ch"),
        P("ctx", "ch"),
        P(None, ("ch", "ctx")),
        P("ch"),
    )
    return jax.shard_map(
        shards,
        mesh=mesh,
        in_specs=placed,
        out_specs=(P("ctx", "ch"), P("ctx", "ch"), P("ctx", "ch"), P("ctx", "ch")),
        check_vma=False,
    )
```
